32 devices in a mesh: groups: 2 (over x), frame: 16 (over z, y, core).
Axes of the slice: x: 2, y: 2, z: 4, core: 2. Of those that a mesh axis runs over, the one named last changes fastest.
Arguments:
- latents: bfloat16 [128, 2, 64, 320], P(('groups', 'frame')), parts along dimension 0, may hold values from -6 to 6
- norm_gain: float32 [320], replicated, may hold values from 0.1 to 1.9
- w_qkv: bfloat16 [320, 960], replicated, may hold values from -0.3125 to 0.3125
- w_out: bfloat16 [320, 320], replicated, may hold values from -0.3125 to 0.3125
- gn_gain: float32 [2, 320], replicated, may hold values from 0.1 to 1.9
- conv_one: bfloat16 [3, 3, 320, 320], replicated, may hold values from -0.109375 to 0.109375
- conv_two: bfloat16 [3, 3, 320, 320], replicated, may hold values from -0.109375 to 0.109375
- step_embed: float32 [320], replicated, may hold values from -4 to 4
- offsets: int32 [32], P('groups'), parts along dimension 0, may hold values from 0 to 3
- numerators: int32 [16], replicated, may hold values from 1 to 16
Outputs:
- result: bfloat16 [128, 2, 64, 320], P(('groups', 'frame')), parts along dimension 0
The draws below stay inside these ranges and needn't reach their ends.
There are 2 independent parts, one for each index of `groups`. The reference program is written for one: setup_inputs(seed, part) draws one part's arguments, and reference() takes and returns one part's arrays. A program takes and returns all parts, laid end to end along the dimension named above; an argument that names none is the same for every part. Nothing has to cross between parts.
All inputs are finite; a program needn't handle non-finite values.
Results may differ from the reference program's by a relative error of at most 0.009.
Values may be sent and summed in bfloat16 or wider, within the bound.
No kernel may reach another device: no remote copies, remote signals or barrier semaphores. Data moves between devices by JAX's collectives and lax.ppermute only.
A program may use at most 64 MiB of HBM per device.

```python
import jax
import jax.numpy as jnp
from jax import lax

C = 320
HEADS = 5
HEAD_DIM = 64
NORM_GROUPS = 32
BLOCK = 4
WINDOW = 16
ROWS = 2
COLS = 64
BLOCKS = 16
FRAMES = 64


def place_ends(result, own_key, low, high):
    dims = result.shape
    place = [jax.random.randint(jax.random.fold_in(own_key, axis), (), 0, dims[axis]) for axis in range(len(dims))]
    result = result.at[tuple(place)].set(low)
    longest = dims.index(max(dims))
    place[longest] = (place[longest] + 1) % dims[longest]
    return result.at[tuple(place)].set(high)


def block_scale(stream_key, dims, shards, low, high):
    level, own = 1.0, jax.random.fold_in(stream_key, 6)
    for axis_at, blocks in shards:
        draws = jnp.exp(jax.random.uniform(jax.random.fold_in(own, axis_at), (blocks,), jnp.float32, low / len(shards), high / len(shards)))
        level = level * jnp.repeat(draws, dims[axis_at] // blocks).reshape([-1 if axis == axis_at else 1 for axis in range(len(dims))])
    return level


def bell_draw(own_key, extent, width, reach, shards=(), held_as=jnp.bfloat16):
    result = jax.random.normal(own_key, extent, jnp.float32) * width
    if len(shards) > 0:
        result = block_scale(own_key, extent, shards, -0.22, 0.18) * result
    return jnp.clip(result, min=-reach, max=reach).astype(held_as)


def setup_inputs(seed: int = 0, part: int = 0) -> dict:
    key_of = jax.random.split(jax.random.key(seed), 11)
    part_splits = jax.random.split(jax.random.fold_in(key_of[10], part), 11)
    return {
        "latents": bell_draw(part_splits[0], (FRAMES, ROWS, COLS, C), 1.0, 6.0, ((0, 16),)),
        "norm_gain": jnp.clip(1.0 + 0.18 * jax.random.normal(key_of[1], (C,), jnp.float32), 0.1, 1.9),
        "w_qkv": bell_draw(key_of[2], (C, 3 * C), C ** -0.5, 0.3125),
        "w_out": bell_draw(key_of[3], (C, C), C ** -0.5, 0.3125),
        "gn_gain": jnp.clip(1.0 + 0.18 * jax.random.normal(key_of[4], (2, C), jnp.float32), 0.1, 1.9),
        "conv_one": bell_draw(key_of[5], (3, 3, C, C), (9 * C) ** -0.5, 0.109375),
        "conv_two": bell_draw(key_of[6], (3, 3, C, C), (9 * C) ** -0.5, 0.109375),
        "step_embed": bell_draw(key_of[7], (C,), 1.0, 4.0, (), jnp.float32),
        "offsets": place_ends(jax.random.randint(part_splits[8], (BLOCKS,), 0, BLOCK), jax.random.fold_in(part_splits[8], 1), 0, BLOCK - 1).astype(jnp.int32),
        "numerators": place_ends(jax.random.randint(key_of[9], (WINDOW,), 1, 17), jax.random.fold_in(key_of[9], 1), 1, 16).astype(jnp.int32),
    }


def layer_project(frames, norm_gain, w_qkv):
    channels = frames.shape[-1]
    values32 = frames.astype(jnp.float32)
    average = lax.optimization_barrier(jnp.mean(values32, axis=-1, keepdims=True))
    centered = values32 - average
    variance = lax.optimization_barrier(jnp.mean(centered * centered, axis=-1, keepdims=True))
    normed = (centered * lax.rsqrt(variance + 1e-05) * norm_gain).astype(jnp.bfloat16)
    qkv = jnp.dot(normed.reshape(-1, channels), w_qkv, preferred_element_type=jnp.float32).astype(jnp.bfloat16)
    return qkv.reshape(frames.shape[0], -1, 3 * channels)

def window_attend(window, numer_f):
    frame_count, pos_count, triple = window.shape
    channels = triple // 3
    queries = window[..., :channels].reshape(frame_count, pos_count, HEADS, HEAD_DIM).astype(jnp.float32)
    keys = window[..., channels:2 * channels].reshape(frame_count, pos_count, HEADS, HEAD_DIM).astype(jnp.float32)
    values = window[..., 2 * channels:].reshape(frame_count, pos_count, HEADS, HEAD_DIM).astype(jnp.float32)
    scores = jnp.einsum('jphd,kphd->phjk', queries, keys) / jnp.sqrt(jnp.float32(HEAD_DIM))
    highest = lax.optimization_barrier(jnp.max(scores, axis=-1, keepdims=True))
    expos = jnp.exp(scores - highest)
    probs = (expos / lax.optimization_barrier(jnp.sum(expos, axis=-1, keepdims=True))).astype(jnp.bfloat16)
    attended = jnp.einsum('phjk,kphd->jphd', probs.astype(jnp.float32), values).reshape(frame_count, pos_count, channels)
    return (attended * numer_f[:, None, None]).astype(jnp.bfloat16)

def group_act(tensor, gain):
    shape = tensor.shape
    grouped = tensor.reshape(shape[0], shape[1], shape[2], NORM_GROUPS, shape[3] // NORM_GROUPS)
    average = lax.optimization_barrier(jnp.mean(grouped, axis=(1, 2, 4), keepdims=True))
    centered = grouped - average
    variance = lax.optimization_barrier(jnp.mean(centered * centered, axis=(1, 2, 4), keepdims=True))
    normed = (centered * lax.rsqrt(variance + 1e-05)).reshape(shape) * gain
    return jax.nn.silu(normed).astype(jnp.bfloat16)

def conv_three(tensor, kernel):
    return lax.conv_general_dilated(tensor.astype(jnp.float32), kernel.astype(jnp.float32), (1, 1), 'SAME', dimension_numbers=('NHWC', 'HWIO', 'NHWC'), preferred_element_type=jnp.float32)

def reference(latents, norm_gain, w_qkv, w_out, gn_gain, conv_one, conv_two, step_embed, offsets, numerators):
    channels = latents.shape[-1]
    qkv = layer_project(latents, norm_gain, w_qkv)
    numer_f = numerators.astype(jnp.float32)
    steps_in = jnp.arange(WINDOW, dtype=jnp.int32)

    def add_window(totals, window_id):
        frame_index = ((BLOCK * window_id + offsets[window_id] + steps_in) % FRAMES).astype(jnp.int32)
        weighted = window_attend(qkv[frame_index], numer_f)
        return (totals.at[frame_index].add(weighted.astype(jnp.float32)), None)
    empty = jnp.zeros((FRAMES, qkv.shape[1], channels), jnp.float32)
    totals, unused = lax.scan(add_window, empty, jnp.arange(BLOCKS, dtype=jnp.int32))
    all_index = ((BLOCK * jnp.arange(BLOCKS, dtype=jnp.int32)[:, None] + offsets[:, None] + steps_in[None, :]) % FRAMES).astype(jnp.int32)
    denominator = jnp.zeros((FRAMES,), jnp.float32).at[all_index.reshape(-1)].add(jnp.tile(numer_f, BLOCKS))
    combined = (totals / denominator[:, None, None]).astype(jnp.bfloat16)
    projected = jnp.dot(combined.reshape(-1, channels), w_out, preferred_element_type=jnp.float32).reshape(latents.shape)
    hidden = (latents.astype(jnp.float32) + projected).astype(jnp.bfloat16)
    first_act = group_act(hidden.astype(jnp.float32), gn_gain[0])
    middle = conv_three(first_act, conv_one) + step_embed
    second_act = group_act(middle, gn_gain[1])
    return (hidden.astype(jnp.float32) + conv_three(second_act, conv_two)).astype(jnp.bfloat16)
```

```python
import functools

import jax
import jax.numpy as jnp
from jax import lax
from jax.experimental import pallas as pl
from jax.experimental.pallas import tpu as pltpu
from jax.sharding import PartitionSpec as P

HEADS = 5
NORM_GROUPS = 32
BLOCK = 4
WINDOW = 16
REACH = WINDOW // BLOCK
EPS = 1e-05
LANES = 128
LOG2E = 1.4426950408889634
NT = (((1,), (1,)), ((), ()))
TN = (((0,), (0,)), ((), ()))


def attend_kernel(
    frames, cells, off_ref, num_ref, x_ref, gain_ref, w_ref, out_ref, qkv_ref, bias_ref, coef_ref, acc_ref
):
    channels = x_ref.shape[-1]
    head_dim = channels // HEADS
    blocks = frames // BLOCK
    wide = HEADS * frames

    x = x_ref[...].astype(jnp.float32)
    cen = x - jnp.mean(x, axis=-1, keepdims=True)
    var = jnp.mean(cen * cen, axis=-1, keepdims=True)
    normed = (cen * lax.rsqrt(var + EPS) * gain_ref[...]).astype(jnp.bfloat16)
    lanes = qkv_ref.shape[-1]
    chunks = acc_ref.shape[0]
    pad = jnp.zeros((x.shape[0], chunks * lanes - channels), jnp.float32)
    for i in range(3):
        part = jnp.dot(
            normed, w_ref[:, i * channels : (i + 1) * channels], preferred_element_type=jnp.float32
        )
        part = jnp.concatenate([part, pad], 1)
        for j in range(chunks):
            qkv_ref[i * chunks + j] = part[:, j * lanes : (j + 1) * lanes]

    frame = lax.broadcasted_iota(jnp.int32, (1, wide), 1) % frames
    block, rest = frame // BLOCK, frame % BLOCK
    key = lax.broadcasted_iota(jnp.int32, (frames, wide), 0)
    weights = []
    for back in range(REACH + 1):
        owner = (block - back + blocks) % blocks
        shift = jnp.zeros((1, wide), jnp.int32)
        for w in range(blocks):
            shift = jnp.where(owner == w, off_ref[w], shift)
        place = BLOCK * back + rest - shift
        weight = jnp.zeros((1, wide), jnp.int32)
        for j in range(WINDOW):
            weight = jnp.where(place == j, num_ref[j], weight)
        weights.append(weight.astype(jnp.float32))
        rel = key - (BLOCK * owner + shift)
        rel = jnp.where(rel < 0, rel + frames, rel)
        bias_ref[back] = jnp.where(rel < WINDOW, 0.0, -1e30)
    total = sum(weights)
    for back in range(REACH + 1):
        coef_ref[back] = weights[back] / total

    lane_head = lax.broadcasted_iota(jnp.int32, (1, chunks * lanes), 1) // head_dim

    def cell_step(p, carry):
        rows = pl.ds(p, frames, stride=cells)
        q, k, v = (
            jnp.concatenate([qkv_ref[i * chunks + j, rows, :] for j in range(chunks)], 1)
            for i in range(3)
        )
        q = q * (head_dim**-0.5)
        k = k.astype(jnp.bfloat16)
        v = v.astype(jnp.bfloat16)
        q_all = jnp.concatenate(
            [jnp.where(lane_head == h, q, 0.0) for h in range(HEADS)], 0
        ).astype(jnp.bfloat16)
        scores = lax.dot_general(k, q_all, NT, preferred_element_type=jnp.float32) * LOG2E
        mixed = jnp.zeros((frames, wide), jnp.float32)
        for back in range(REACH + 1):
            s = scores + bias_ref[back]
            e = jnp.exp2(s - jnp.max(s, axis=0, keepdims=True))
            z = jnp.sum(e, axis=0, keepdims=True)
            mixed = mixed + e * (coef_ref[back] / z)
        full = lax.dot_general(
            mixed.astype(jnp.bfloat16), v, TN, preferred_element_type=jnp.float32
        )
        out = full[:frames]
        for h in range(1, HEADS):
            out = jnp.where(lane_head == h, full[h * frames : (h + 1) * frames], out)
        for j in range(chunks):
            acc_ref[j, rows, :] = out[:, j * lanes : (j + 1) * lanes]
        return carry

    for p in range(cells):
        cell_step(p, 0)
    gathered = jnp.concatenate([acc_ref[j] for j in range(chunks)], 1)
    out_ref[...] = gathered[:, :channels].astype(out_ref.dtype)


def attend(x, norm_gain, w_qkv, offsets, numerators, frames, cells):
    channels = x.shape[-1]
    vmem = pl.BlockSpec(memory_space=pltpu.VMEM)
    smem = pl.BlockSpec(memory_space=pltpu.SMEM)
    rows = frames * cells
    wide = HEADS * frames
    chunks = -(-channels // LANES)
    return pl.pallas_call(
        functools.partial(attend_kernel, frames, cells),
        out_shape=jax.ShapeDtypeStruct((rows, channels), jnp.bfloat16),
        in_specs=[smem, smem, vmem, vmem, vmem],
        out_specs=vmem,
        scratch_shapes=[
            pltpu.VMEM((3 * chunks, rows, LANES), jnp.float32),
            pltpu.VMEM((REACH + 1, frames, wide), jnp.float32),
            pltpu.VMEM((REACH + 1, 1, wide), jnp.float32),
            pltpu.VMEM((chunks, rows, LANES), jnp.float32),
        ],
        compiler_params=pltpu.CompilerParams(vmem_limit_bytes=40 * 1024 * 1024),
        name="window_attention",
    )(offsets, numerators, x, norm_gain.reshape(1, channels), w_qkv)


def group_mean(sums, spread, count):
    high = sums.astype(jnp.bfloat16)
    left = sums - high.astype(jnp.float32)
    mid = left.astype(jnp.bfloat16)
    low = (left - mid.astype(jnp.float32)).astype(jnp.bfloat16)
    dot = functools.partial(jnp.dot, preferred_element_type=jnp.float32)
    return (dot(high, spread) + dot(mid, spread) + dot(low, spread)) * (1.0 / count)


def group_act(rows, gain, spread, count):
    sums = sum(jnp.sum(row, axis=1) for row in rows)
    average = group_mean(sums, spread, count)
    cens = [row - average[:, None, :] for row in rows]
    variance = group_mean(sum(jnp.sum(cen * cen, axis=1) for cen in cens), spread, count)
    scale = lax.rsqrt(variance + EPS) * gain
    acts = []
    for cen in cens:
        v = cen * scale[:, None, :]
        acts.append(v / (1.0 + jnp.exp(-v)))
    return acts


def conv_rows(acts, w_ref, taps_ref):
    frames, cols, channels = acts[0].shape
    deep = w_ref.shape[1]
    count = len(acts)
    col = lax.broadcasted_iota(jnp.int32, (frames * cols, 1), 0) % cols
    for r, act in enumerate(acts):
        flat = act.reshape(frames * cols, channels)
        before = jnp.where(col == 0, 0.0, pltpu.roll(flat, 1, 0))
        after = jnp.where(col == cols - 1, 0.0, pltpu.roll(flat, frames * cols - 1, 0))
        for kw, part in enumerate((before, flat, after)):
            start = (3 * r + kw) * deep
            taps_ref[:, start : start + channels] = part.astype(jnp.bfloat16)
    outs = []
    for r in range(count):
        lo, hi = max(r - 1, 0), min(r + 1, count - 1)
        left = taps_ref[:, 3 * lo * deep : 3 * (hi + 1) * deep]
        right = w_ref[3 * (lo - r + 1) : 3 * (hi - r + 2)]
        right = right.reshape(-1, channels)
        out = jnp.dot(left, right, preferred_element_type=jnp.float32)
        outs.append(out.reshape(frames, cols, channels))
    return outs


def res_kernel(
    comb_ref, lat_ref, w_out_ref, gn_ref, step_ref, one_hbm, two_hbm, out_ref, one_ref, two_ref, taps_ref, sem
):
    frames, count, cols, channels = lat_ref.shape
    deep = one_ref.shape[1]
    copies = []
    for i, (src, dst) in enumerate(((one_hbm, one_ref), (two_hbm, two_ref))):
        copy = pltpu.make_async_copy(src, dst.at[:, :channels, :], sem.at[i])
        copy.start()
        copies.append(copy)
    for ref in (one_ref, two_ref):
        ref[:, channels:, :] = jnp.zeros((ref.shape[0], deep - channels, channels), jnp.bfloat16)
    for i in range(3 * count):
        taps_ref[:, i * deep + channels : (i + 1) * deep] = jnp.zeros(
            (frames * cols, deep - channels), jnp.bfloat16
        )
    size = channels // NORM_GROUPS
    group_r = lax.broadcasted_iota(jnp.int32, (channels, channels), 0) // size
    group_c = lax.broadcasted_iota(jnp.int32, (channels, channels), 1) // size
    spread = jnp.where(group_r == group_c, 1.0, 0.0).astype(jnp.bfloat16)
    members = count * cols * size

    hidden = []
    for r in range(count):
        comb = comb_ref[:, r * cols : (r + 1) * cols, :].reshape(frames * cols, channels)
        proj = jnp.dot(comb, w_out_ref[...], preferred_element_type=jnp.float32)
        hid = lat_ref[:, r].astype(jnp.float32) + proj.reshape(frames, cols, channels)
        hidden.append(hid.astype(jnp.bfloat16).astype(jnp.float32))
    acts = group_act(hidden, gn_ref[0:1], spread, members)
    copies[0].wait()
    middle = [row + step_ref[...][None] for row in conv_rows(acts, one_ref, taps_ref)]
    acts = group_act(middle, gn_ref[1:2], spread, members)
    copies[1].wait()
    for r, row in enumerate(conv_rows(acts, two_ref, taps_ref)):
        out_ref[:, r] = (hidden[r] + row).astype(out_ref.dtype)


def res_block(combined, latents, w_out, gn_gain, conv_one, conv_two, step_embed):
    frames, count, cols, channels = latents.shape
    deep = -(-channels // 128) * 128
    vmem = pl.BlockSpec(memory_space=pltpu.VMEM)
    hbm = pl.BlockSpec(memory_space=pl.ANY)
    return pl.pallas_call(
        res_kernel,
        out_shape=jax.ShapeDtypeStruct(latents.shape, jnp.bfloat16),
        in_specs=[vmem] * 5 + [hbm] * 2,
        out_specs=vmem,
        scratch_shapes=[
            pltpu.VMEM((9, deep, channels), jnp.bfloat16),
            pltpu.VMEM((9, deep, channels), jnp.bfloat16),
            pltpu.VMEM((frames * cols, 3 * count * deep), jnp.bfloat16),
            pltpu.SemaphoreType.DMA((2,)),
        ],
        compiler_params=pltpu.CompilerParams(vmem_limit_bytes=32 * 1024 * 1024),
        name="res_block",
    )(
        combined,
        latents,
        w_out,
        gn_gain,
        step_embed.reshape(1, channels),
        conv_one.reshape(9, channels, channels),
        conv_two.reshape(9, channels, channels),
    )


def body(
    latents, norm_gain, w_qkv, w_out, gn_gain, conv_one, conv_two, step_embed, offsets, numerators
):
    block_len, tile_rows, tile_cols, channels = latents.shape
    count = lax.axis_size("frame")
    cells = tile_rows * tile_cols // count
    frames = block_len * count
    local = latents.reshape(block_len, tile_rows * tile_cols, channels)
    spread = lax.all_to_all(local, "frame", 1, 0, tiled=True)
    combined = attend(
        spread.reshape(frames * cells, channels), norm_gain, w_qkv, offsets, numerators, frames, cells
    )
    combined = lax.all_to_all(
        combined.reshape(frames, cells, channels), "frame", 0, 1, tiled=True
    )
    return res_block(combined, latents, w_out, gn_gain, conv_one, conv_two, step_embed)


def solution(mesh):
    return jax.shard_map(
        body,
        mesh=mesh,
        in_specs=(
            P(("groups", "frame"), None, None, None),
            P(),
            P(),
            P(),
            P(),
            P(),
            P(),
            P(),
            P("groups"),
            P(),
        ),
        out_specs=P(("groups", "frame"), None, None, None),
        check_vma=False,
    )
```

```python
import functools

import jax
import jax.numpy as jnp
from jax import lax
from jax.experimental import pallas as pl
from jax.experimental.pallas import tpu as pltpu
from jax.sharding import PartitionSpec as P

HEADS = 5
NORM_GROUPS = 32
BLOCK = 4
WINDOW = 16
REACH = WINDOW // BLOCK
EPS = 1e-05
LANES = 128
GROUP = 4
LOG2E = 1.4426950408889634
NT = (((1,), (1,)), ((), ()))
QUARTERS = 4
PACK = 2


def place():
    me = lax.axis_index("frame")
    return me % 2, me // 2 % 2, me // QUARTERS


def moved(array, target):
    count = lax.axis_size("frame")
    return lax.ppermute(array, "frame", [(i, target(i) % count) for i in range(count)])


def pack_kernel(lat_ref, mine_ref, theirs_ref):
    core, chip, _ = place()
    frames, _, cells, channels = lat_ref.shape
    half = cells // PACK
    for out_ref, side in ((mine_ref, core), (theirs_ref, 1 - core)):
        for i, tall in enumerate((chip, 1 - chip)):
            x = lat_ref[:, side * 2 + tall]
            x = jnp.concatenate([x[:, :half], x[:, half:]], -1)
            out_ref[i] = x.reshape(frames * half, PACK * channels)


def join_kernel(mine_ref, other_ref, near_ref, far_ref):
    rows = mine_ref.shape[1]
    for i, out_ref in enumerate((near_ref, far_ref)):
        out_ref[:rows] = mine_ref[i]
        out_ref[rows:] = other_ref[i]


def attend_kernel(
    cells, planes, off_ref, num_ref, *refs
):
    parts = refs[:6]
    gain_ref, w_ref, own_ref, sib_ref, far_own_ref, far_sib_ref = refs[6:12]
    norm_ref, q_ref, k_ref, v_ref, bias_ref, coef_ref, acc_ref = refs[12:]
    core, chip, plane = place()
    channels = w_ref.shape[0]
    head_dim = channels // HEADS
    half = cells // PACK
    part_rows = parts[0].shape[0]
    part_frames = part_rows // half
    key_frames, query_frames = part_frames * 6, part_frames * 2
    key_rows, query_rows = key_frames * half, query_frames * half
    blocks = planes * QUARTERS
    frames = blocks * BLOCK
    group = GROUP
    wide = group * HEADS * query_frames
    chunks, lanes = k_ref.shape[0], k_ref.shape[2]

    for b, part in enumerate(parts):
        for a in range(PACK):
            x = part[:, a * channels : (a + 1) * channels].astype(jnp.float32)
            cen = x - jnp.mean(x, axis=-1, keepdims=True)
            var = jnp.mean(cen * cen, axis=-1, keepdims=True)
            start = a * key_rows + b * part_rows
            norm_ref[start : start + part_rows] = (
                cen * lax.rsqrt(var + EPS) * gain_ref[...]
            ).astype(jnp.bfloat16)
    pad = jnp.zeros((channels, chunks * lanes - channels), jnp.bfloat16)
    for i, (out_ref, rows) in enumerate(((q_ref, query_rows), (k_ref, key_rows), (v_ref, key_rows))):
        w = jnp.concatenate([w_ref[:, i * channels : (i + 1) * channels], pad], 1)
        for a in range(PACK):
            here = norm_ref[a * key_rows : a * key_rows + rows]
            res = jnp.dot(here, w, preferred_element_type=jnp.float32)
            for j in range(chunks):
                out_ref[j, a * rows : (a + 1) * rows] = res[:, j * lanes : (j + 1) * lanes]

    ids = []
    for step in (0, planes - 1, 1):
        for tall in (chip, 1 - chip):
            base = lax.rem(plane + step, planes) * QUARTERS + 2 * tall
            ids += [base + core, base + 1 - core]
    lane = lax.broadcasted_iota(jnp.int32, (1, wide), 1)
    query = lane % query_frames
    block = jnp.zeros((1, wide), jnp.int32)
    for i in range(query_frames // BLOCK):
        block = jnp.where(query // BLOCK == i, ids[i], block)
    rest = query % BLOCK
    spot = lax.broadcasted_iota(jnp.int32, (key_frames, wide), 0)
    key = jnp.zeros((key_frames, wide), jnp.int32)
    for i, at in enumerate(ids):
        key = jnp.where(spot // BLOCK == i, at * BLOCK, key)
    key = key + spot % BLOCK
    weights = []
    for back in range(REACH + 1):
        owner = block - back
        owner = jnp.where(owner < 0, owner + blocks, owner)
        shift = jnp.zeros((1, wide), jnp.int32)
        for w in range(blocks):
            shift = jnp.where(owner == w, off_ref[w], shift)
        at = BLOCK * back + rest - shift
        weight = jnp.zeros((1, wide), jnp.int32)
        for j in range(WINDOW):
            weight = jnp.where(at == j, num_ref[j], weight)
        weights.append(weight.astype(jnp.float32))
        rel = key - (BLOCK * owner + shift)
        rel = jnp.where(rel < 0, rel + frames, rel)
        bias_ref[back] = jnp.where(rel < WINDOW, 0.0, -1e30)
    total = sum(weights)
    for back in range(REACH + 1):
        coef_ref[back] = weights[back] / total

    lane_head = lax.broadcasted_iota(jnp.int32, (1, chunks * lanes), 1) // head_dim
    lane_cell = lane // (HEADS * query_frames)
    span = HEADS * query_frames

    def rows_of(ref, start, size):
        rows = pl.ds(start, size, stride=half)
        return jnp.concatenate([ref[j, rows, :] for j in range(chunks)], 1)

    def group_step(a, first):
        keys, values, queries = [], [], []
        for g in range(group):
            at = first + g
            keys.append(rows_of(k_ref, a * key_rows + at, key_frames).astype(jnp.bfloat16))
            values.append(rows_of(v_ref, a * key_rows + at, key_frames).astype(jnp.bfloat16))
            q = rows_of(q_ref, a * query_rows + at, query_frames) * (head_dim**-0.5)
            queries += [jnp.where(lane_head == h, q, 0.0) for h in range(HEADS)]
        keys = jnp.concatenate(keys, 0)
        queries = jnp.concatenate(queries, 0).astype(jnp.bfloat16)
        cross = lax.dot_general(keys, queries, NT, preferred_element_type=jnp.float32)
        scores = cross[:key_frames]
        for g in range(1, group):
            scores = jnp.where(lane_cell == g, cross[g * key_frames : (g + 1) * key_frames], scores)
        scores = scores * LOG2E
        mixed = jnp.zeros((key_frames, wide), jnp.float32)
        for back in range(REACH + 1):
            s = scores + bias_ref[back]
            e = jnp.exp2(s - jnp.max(s, axis=0, keepdims=True))
            z = jnp.sum(e, axis=0, keepdims=True)
            mixed = mixed + e * (coef_ref[back] / z)
        mixed = mixed.T.astype(jnp.bfloat16)
        for g in range(group):
            full = jnp.dot(
                mixed[g * span : (g + 1) * span], values[g], preferred_element_type=jnp.float32
            )
            out = full[:query_frames]
            for h in range(1, HEADS):
                out = jnp.where(lane_head == h, full[h * query_frames : (h + 1) * query_frames], out)
            rows = pl.ds(a * query_rows + first + g, query_frames, stride=half)
            for j in range(chunks):
                acc_ref[j, rows, :] = out[:, j * lanes : (j + 1) * lanes]

    for a in range(PACK):
        for first in range(0, half, group):
            group_step(a, first)
    quarter = query_rows // 4
    for i, out_ref in enumerate((own_ref, sib_ref, far_own_ref, far_sib_ref)):
        pieces = []
        for a in range(PACK):
            start = a * query_rows + i * quarter
            piece = jnp.concatenate([acc_ref[j, start : start + quarter] for j in range(chunks)], 1)
            pieces.append(piece[:, :channels])
        out_ref[...] = jnp.concatenate(pieces, 1).astype(out_ref.dtype)


def attend(parts, norm_gain, w_qkv, offsets, numerators, cells, planes):
    channels = w_qkv.shape[0]
    vmem = pl.BlockSpec(memory_space=pltpu.VMEM)
    smem = pl.BlockSpec(memory_space=pltpu.SMEM)
    rows, packed = parts[0].shape
    chunks = -(-channels // LANES)
    query_frames = 2 * rows * PACK // cells
    wide = GROUP * HEADS * query_frames
    keys, queries = 6 * rows * PACK, 2 * rows * PACK
    return pl.pallas_call(
        functools.partial(attend_kernel, cells, planes),
        out_shape=[jax.ShapeDtypeStruct((rows // 2, packed), jnp.bfloat16)] * 4,
        in_specs=[smem, smem] + [vmem] * 8,
        out_specs=[vmem] * 4,
        scratch_shapes=[
            pltpu.VMEM((keys, channels), jnp.bfloat16),
            pltpu.VMEM((chunks, queries, LANES), jnp.float32),
            pltpu.VMEM((chunks, keys, LANES), jnp.float32),
            pltpu.VMEM((chunks, keys, LANES), jnp.float32),
            pltpu.VMEM((REACH + 1, 3 * query_frames, wide), jnp.float32),
            pltpu.VMEM((REACH + 1, 1, wide), jnp.float32),
            pltpu.VMEM((chunks, queries, LANES), jnp.float32),
        ],
        compiler_params=pltpu.CompilerParams(vmem_limit_bytes=24 * 1024 * 1024),
        name="window_attention",
    )(offsets, numerators, *parts, norm_gain.reshape(1, channels), w_qkv)


def group_mean(sums, spread, count):
    high = sums.astype(jnp.bfloat16)
    left = sums - high.astype(jnp.float32)
    mid = left.astype(jnp.bfloat16)
    low = (left - mid.astype(jnp.float32)).astype(jnp.bfloat16)
    dot = functools.partial(jnp.dot, preferred_element_type=jnp.float32)
    return (dot(high, spread) + dot(mid, spread) + dot(low, spread)) * (1.0 / count)


def group_act(rows, gain, spread, count):
    sums = sum(jnp.sum(row, axis=1) for row in rows)
    average = group_mean(sums, spread, count)
    cens = [row - average[:, None, :] for row in rows]
    variance = group_mean(sum(jnp.sum(cen * cen, axis=1) for cen in cens), spread, count)
    scale = lax.rsqrt(variance + EPS) * gain
    acts = []
    for cen in cens:
        v = cen * scale[:, None, :]
        acts.append(v / (1.0 + jnp.exp(-v)))
    return acts


def conv_rows(acts, w_ref, taps_ref):
    frames, cols, channels = acts[0].shape
    deep = w_ref.shape[1]
    count = len(acts)
    col = lax.broadcasted_iota(jnp.int32, (frames * cols, 1), 0) % cols
    for r, act in enumerate(acts):
        flat = act.reshape(frames * cols, channels)
        before = jnp.where(col == 0, 0.0, pltpu.roll(flat, 1, 0))
        after = jnp.where(col == cols - 1, 0.0, pltpu.roll(flat, frames * cols - 1, 0))
        for kw, part in enumerate((before, flat, after)):
            start = (3 * r + kw) * deep
            taps_ref[:, start : start + channels] = part.astype(jnp.bfloat16)
    outs = []
    for r in range(count):
        lo, hi = max(r - 1, 0), min(r + 1, count - 1)
        left = taps_ref[:, 3 * lo * deep : 3 * (hi + 1) * deep]
        right = w_ref[3 * (lo - r + 1) : 3 * (hi - r + 2)]
        right = right.reshape(-1, channels)
        out = jnp.dot(left, right, preferred_element_type=jnp.float32)
        outs.append(out.reshape(frames, cols, channels))
    return outs


def res_kernel(
    p0_ref, p1_ref, p2_ref, p3_ref, lat_ref, w_out_ref, gn_ref, step_ref, one_hbm, two_hbm, out_ref,
    comb_ref, one_ref, two_ref, taps_ref, sem
):
    frames, count, cols, channels = lat_ref.shape
    deep = one_ref.shape[1]
    copies = []
    for i, (src, dst) in enumerate(((one_hbm, one_ref), (two_hbm, two_ref))):
        copy = pltpu.make_async_copy(src, dst.at[:, :channels, :], sem.at[i])
        copy.start()
        copies.append(copy)
    for ref in (one_ref, two_ref):
        ref[:, channels:, :] = jnp.zeros((ref.shape[0], deep - channels, channels), jnp.bfloat16)
    for i in range(3 * count):
        taps_ref[:, i * deep + channels : (i + 1) * deep] = jnp.zeros(
            (frames * cols, deep - channels), jnp.bfloat16
        )
    size = channels // NORM_GROUPS
    group_r = lax.broadcasted_iota(jnp.int32, (channels, channels), 0) // size
    group_c = lax.broadcasted_iota(jnp.int32, (channels, channels), 1) // size
    spread = jnp.where(group_r == group_c, 1.0, 0.0).astype(jnp.bfloat16)
    members = count * cols * size

    core, chip, _ = place()
    half = comb_ref.shape[2] // PACK
    for part, side, tall in (
        (p0_ref, core, chip), (p1_ref, 1 - core, chip), (p2_ref, core, 1 - chip), (p3_ref, 1 - core, 1 - chip)
    ):
        for a in range(PACK):
            piece = part[:, a * channels : (a + 1) * channels].reshape(frames, half, channels)
            comb_ref[:, side * 2 + tall, a * half : (a + 1) * half, :] = piece
    combined = comb_ref[...].reshape(frames, count * cols, channels)
    hidden = []
    for r in range(count):
        comb = combined[:, r * cols : (r + 1) * cols, :].reshape(frames * cols, channels)
        proj = jnp.dot(comb, w_out_ref[...], preferred_element_type=jnp.float32)
        hid = lat_ref[:, r].astype(jnp.float32) + proj.reshape(frames, cols, channels)
        hidden.append(hid.astype(jnp.bfloat16).astype(jnp.float32))
    acts = group_act(hidden, gn_ref[0:1], spread, members)
    copies[0].wait()
    middle = [row + step_ref[...][None] for row in conv_rows(acts, one_ref, taps_ref)]
    acts = group_act(middle, gn_ref[1:2], spread, members)
    copies[1].wait()
    for r, row in enumerate(conv_rows(acts, two_ref, taps_ref)):
        out_ref[:, r] = (hidden[r] + row).astype(out_ref.dtype)


def res_block(parts, latents, w_out, gn_gain, conv_one, conv_two, step_embed):
    frames, count, cols, channels = latents.shape
    deep = -(-channels // 128) * 128
    vmem = pl.BlockSpec(memory_space=pltpu.VMEM)
    hbm = pl.BlockSpec(memory_space=pltpu.HBM)
    return pl.pallas_call(
        res_kernel,
        out_shape=jax.ShapeDtypeStruct(latents.shape, jnp.bfloat16),
        in_specs=[vmem] * 8 + [hbm] * 2,
        out_specs=vmem,
        scratch_shapes=[
            pltpu.VMEM((frames, QUARTERS, count * cols // QUARTERS, channels), jnp.bfloat16),
            pltpu.VMEM((9, deep, channels), jnp.bfloat16),
            pltpu.VMEM((9, deep, channels), jnp.bfloat16),
            pltpu.VMEM((frames * cols, 3 * count * deep), jnp.bfloat16),
            pltpu.SemaphoreType.DMA((2,)),
        ],
        compiler_params=pltpu.CompilerParams(vmem_limit_bytes=24 * 1024 * 1024),
        name="res_block",
    )(
        *parts,
        latents,
        w_out,
        gn_gain,
        step_embed.reshape(1, channels),
        conv_one.reshape(9, channels, channels),
        conv_two.reshape(9, channels, channels),
    )


def body(
    latents, norm_gain, w_qkv, w_out, gn_gain, conv_one, conv_two, step_embed, offsets, numerators
):
    block_len, tile_rows, tile_cols, channels = latents.shape
    planes = lax.axis_size("frame") // QUARTERS
    cells = tile_rows * tile_cols // QUARTERS
    vmem = pl.BlockSpec(memory_space=pltpu.VMEM)
    rows, packed = block_len * cells // PACK, PACK * channels
    mine, theirs = pl.pallas_call(
        pack_kernel,
        out_shape=[jax.ShapeDtypeStruct((2, rows, packed), jnp.bfloat16)] * 2,
        in_specs=[vmem],
        out_specs=[vmem] * 2,
        name="pack",
    )(latents.reshape(block_len, QUARTERS, cells, channels))
    other = moved(theirs, lambda i: i ^ 1)
    near, far = pl.pallas_call(
        join_kernel,
        out_shape=[jax.ShapeDtypeStruct((2 * rows, packed), jnp.bfloat16)] * 2,
        in_specs=[vmem] * 2,
        out_specs=[vmem] * 2,
        name="join",
    )(mine, other)
    parts = [
        near,
        moved(far, lambda i: i ^ 2),
        moved(near, lambda i: i + QUARTERS),
        moved(far, lambda i: (i ^ 2) + QUARTERS),
        moved(near, lambda i: i - QUARTERS),
        moved(far, lambda i: (i ^ 2) - QUARTERS),
    ]
    own, sib, far_own, far_sib = attend(
        parts, norm_gain, w_qkv, offsets, numerators, cells, planes
    )
    pieces = [
        own,
        moved(sib, lambda i: i ^ 1),
        moved(far_own, lambda i: i ^ 2),
        moved(moved(far_sib, lambda i: i ^ 1), lambda i: i ^ 2),
    ]
    return res_block(pieces, latents, w_out, gn_gain, conv_one, conv_two, step_embed)


def solution(mesh):
    return jax.shard_map(
        body,
        mesh=mesh,
        in_specs=(
            P(("groups", "frame"), None, None, None),
            P(),
            P(),
            P(),
            P(),
            P(),
            P(),
            P(),
            P("groups"),
            P(),
        ),
        out_specs=P(("groups", "frame"), None, None, None),
        check_vma=False,
    )
```

```python
import functools

import jax
import jax.numpy as jnp
from jax import lax
from jax.experimental import pallas as pl
from jax.experimental.pallas import tpu as pltpu
from jax.sharding import PartitionSpec as P

HEADS = 5
NORM_GROUPS = 32
BLOCK = 4
WINDOW = 16
REACH = WINDOW // BLOCK
EPS = 1e-05
LANES = 128
GROUP = 2
LOG2E = 1.4426950408889634
NT = (((1,), (1,)), ((), ()))
QUARTERS = 4
PACK = 2


def place():
    me = lax.axis_index("frame")
    return me % 2, me // 2 % 2, me // QUARTERS


def moved(array, target):
    count = lax.axis_size("frame")
    return lax.ppermute(array, "frame", [(i, target(i) % count) for i in range(count)])


def pack_lanes(first, second):
    low = lax.broadcasted_iota(jnp.int32, first[-1].shape, first[-1].ndim - 1) < LANES // 2
    tail = jnp.where(low, first[-1], pltpu.roll(second[-1], LANES // 2, second[-1].ndim - 1))
    return jnp.concatenate(first[:-1] + second[:-1] + [tail], -1)


def unpack_lanes(rows):
    chunks = [rows[:, i : i + LANES] for i in range(0, rows.shape[1], LANES)]
    full = len(chunks) // 2
    low = lax.broadcasted_iota(jnp.int32, chunks[-1].shape, 1) < LANES // 2
    first = chunks[:full] + [jnp.where(low, chunks[-1], 0.0)]
    second = chunks[full:-1] + [jnp.where(low, pltpu.roll(chunks[-1], LANES // 2, 1), 0.0)]
    return first, second


def fetch(pairs, sem):
    copies = [pltpu.make_async_copy(src, dst, sem.at[i]) for i, (src, dst) in enumerate(pairs)]
    for copy in copies:
        copy.start()
    return copies


def pack_kernel(lat_ref, near_ref, far_ref):
    core, chip, _ = place()
    frames, _, cells, channels = lat_ref.shape
    half = cells // PACK
    width = -(-channels // LANES) * LANES
    for out_ref, tall in ((near_ref, chip), (far_ref, 1 - chip)):
        for i, side in enumerate((core, 1 - core)):
            x = lat_ref[:, side * 2 + tall].astype(jnp.float32)
            x = jnp.concatenate([x, jnp.zeros((frames, cells, width - channels), x.dtype)], -1)
            halves = []
            for a in range(PACK):
                rows = x[:, a * half : (a + 1) * half].reshape(frames * half, width)
                halves.append([rows[:, j : j + LANES] for j in range(0, width, LANES)])
            out_ref[i] = pack_lanes(*halves).astype(out_ref.dtype)


def attend_kernel(cells, planes, *refs):
    sources, refs = refs[:12], refs[12:]
    off_hbm, num_hbm, gain_hbm, w_hbm, own_ref, sib_ref, far_own_ref, far_sib_ref = refs[:8]
    (
        off_ref, num_ref, gain_ref, w_ref, part_ref, norm_ref, q_ref, k_ref, v_ref, bias_ref, coef_ref, acc_ref, sem,
    ) = refs[8:]
    core, chip, plane = place()
    channels = w_ref.shape[0]
    head_dim = channels // HEADS
    half = cells // PACK
    part_rows = part_ref.shape[1]
    part_frames = part_rows // half
    key_frames, query_frames = part_frames * 12, part_frames * 4
    key_rows, query_rows = key_frames * half, query_frames * half
    blocks = planes * QUARTERS
    frames = blocks * BLOCK
    group = GROUP
    wide = group * HEADS * query_frames
    chunks, lanes = k_ref.shape[0], k_ref.shape[2]
    copies = fetch(
        [(gain_hbm, gain_ref)]
        + [(src.at[i % 2], part_ref.at[i]) for i, src in enumerate(sources)]
        + [(w_hbm, w_ref), (off_hbm, off_ref), (num_hbm, num_ref)],
        sem,
    )

    copies[0].wait()
    gain = gain_ref[...]
    pad = jnp.zeros((1, chunks * lanes - channels), jnp.float32)
    gain = jnp.concatenate([gain, pad], 1)
    last = lax.broadcasted_iota(jnp.int32, (part_rows, lanes), 1) < channels - (chunks - 1) * lanes
    for i in range(len(sources)):
        copies[1 + i].wait()
        for a, x in enumerate(unpack_lanes(part_ref[i].astype(jnp.float32))):
            average = jnp.sum(sum(x), axis=-1, keepdims=True) * (1.0 / channels)
            cen = [chunk - average for chunk in x]
            cen[-1] = jnp.where(last, cen[-1], 0.0)
            var = jnp.sum(sum(chunk * chunk for chunk in cen), axis=-1, keepdims=True)
            scale = lax.rsqrt(var * (1.0 / channels) + EPS)
            start = a * key_rows + i * part_rows
            normed = [
                chunk * scale * gain[:, j * lanes : (j + 1) * lanes] for j, chunk in enumerate(cen)
            ]
            norm_ref[start : start + part_rows] = jnp.concatenate(normed, 1).astype(jnp.bfloat16)
    for copy in copies[1 + len(sources) :]:
        copy.wait()
    pad = jnp.zeros((channels, chunks * lanes - channels), jnp.bfloat16)
    below = jnp.zeros((chunks * lanes - channels, chunks * lanes), jnp.bfloat16)
    for i, (out_ref, rows) in enumerate(((q_ref, query_rows), (k_ref, key_rows), (v_ref, key_rows))):
        w = jnp.concatenate([w_ref[:, i * channels : (i + 1) * channels], pad], 1)
        w = jnp.concatenate([w, below], 0)
        for a in range(PACK):
            here = norm_ref[a * key_rows : a * key_rows + rows]
            res = jnp.dot(here, w, preferred_element_type=jnp.float32)
            for j in range(chunks):
                out_ref[j, a * rows : (a + 1) * rows] = res[:, j * lanes : (j + 1) * lanes]

    ids = []
    for step in (0, planes - 1, 1):
        for tall in (chip, 1 - chip):
            base = lax.rem(plane + step, planes) * QUARTERS + 2 * tall
            ids += [base + core, base + 1 - core]
    lane = lax.broadcasted_iota(jnp.int32, (1, wide), 1)
    query = lane % query_frames
    block = jnp.zeros((1, wide), jnp.int32)
    for i in range(query_frames // BLOCK):
        block = jnp.where(query // BLOCK == i, ids[i], block)
    rest = query % BLOCK
    spot = lax.broadcasted_iota(jnp.int32, (key_frames, wide), 0)
    key = jnp.zeros((key_frames, wide), jnp.int32)
    for i, at in enumerate(ids):
        key = jnp.where(spot // BLOCK == i, at * BLOCK, key)
    key = key + spot % BLOCK
    weights = []
    for back in range(REACH + 1):
        owner = block - back
        owner = jnp.where(owner < 0, owner + blocks, owner)
        shift = jnp.zeros((1, wide), jnp.int32)
        for w in range(blocks):
            shift = jnp.where(owner == w, off_ref[w], shift)
        at = BLOCK * back + rest - shift
        weight = jnp.zeros((1, wide), jnp.int32)
        for j in range(WINDOW):
            weight = jnp.where(at == j, num_ref[j], weight)
        weights.append(weight.astype(jnp.float32))
        rel = key - (BLOCK * owner + shift)
        rel = jnp.where(rel < 0, rel + frames, rel)
        bias_ref[back] = jnp.where(rel < WINDOW, 0.0, -1e30)
    total = sum(weights)
    for back in range(REACH + 1):
        coef_ref[back] = weights[back] / total

    lane_head = lax.broadcasted_iota(jnp.int32, (1, chunks * lanes), 1) // head_dim
    lane_cell = lane // (HEADS * query_frames)
    span = HEADS * query_frames

    def rows_of(ref, start, size):
        rows = pl.ds(start, size, stride=half)
        return jnp.concatenate([ref[j, rows, :] for j in range(chunks)], 1)

    def group_step(a, first):
        keys, values, queries = [], [], []
        for g in range(group):
            at = first + g
            keys.append(rows_of(k_ref, a * key_rows + at, key_frames).astype(jnp.bfloat16))
            values.append(rows_of(v_ref, a * key_rows + at, key_frames).astype(jnp.bfloat16))
            q = rows_of(q_ref, a * query_rows + at, query_frames) * (head_dim**-0.5)
            queries += [jnp.where(lane_head == h, q, 0.0) for h in range(HEADS)]
        keys = jnp.concatenate(keys, 0)
        queries = jnp.concatenate(queries, 0).astype(jnp.bfloat16)
        cross = lax.dot_general(keys, queries, NT, preferred_element_type=jnp.float32)
        scores = cross[:key_frames]
        for g in range(1, group):
            scores = jnp.where(lane_cell == g, cross[g * key_frames : (g + 1) * key_frames], scores)
        scores = scores * LOG2E
        mixed = jnp.zeros((key_frames, wide), jnp.float32)
        for back in range(REACH + 1):
            s = scores + bias_ref[back]
            e = jnp.exp2(s - jnp.max(s, axis=0, keepdims=True))
            z = jnp.sum(e, axis=0, keepdims=True)
            mixed = mixed + e * (coef_ref[back] / z)
        mixed = mixed.T.astype(jnp.bfloat16)
        for g in range(group):
            full = jnp.dot(
                mixed[g * span : (g + 1) * span], values[g], preferred_element_type=jnp.float32
            )
            out = full[:query_frames]
            for h in range(1, HEADS):
                out = jnp.where(lane_head == h, full[h * query_frames : (h + 1) * query_frames], out)
            rows = pl.ds(a * query_rows + first + g, query_frames, stride=half)
            for j in range(chunks):
                acc_ref[j, rows, :] = out[:, j * lanes : (j + 1) * lanes]

    for a in range(PACK):
        for first in range(0, half, group):
            group_step(a, first)
    quarter = query_rows // 4
    for i, out_ref in enumerate((own_ref, sib_ref, far_own_ref, far_sib_ref)):
        pieces = []
        for a in range(PACK):
            start = a * query_rows + i * quarter
            pieces.append([acc_ref[j, start : start + quarter] for j in range(chunks)])
        out_ref[...] = pack_lanes(*pieces).astype(out_ref.dtype)


def attend(parts, norm_gain, w_qkv, offsets, numerators, cells, planes):
    channels = w_qkv.shape[0]
    vmem = pl.BlockSpec(memory_space=pltpu.VMEM)
    _, rows, packed = parts[0].shape
    chunks = -(-channels // LANES)
    query_frames = 4 * rows * PACK // cells
    wide = GROUP * HEADS * query_frames
    keys, queries = 12 * rows * PACK, 4 * rows * PACK
    return pl.pallas_call(
        functools.partial(attend_kernel, cells, planes),
        out_shape=[jax.ShapeDtypeStruct((rows, packed), jnp.bfloat16)] * 4,
        in_specs=[pl.BlockSpec(memory_space=pl.ANY)] * 16,
        out_specs=[vmem] * 4,
        scratch_shapes=[
            pltpu.SMEM(offsets.shape, jnp.int32),
            pltpu.SMEM(numerators.shape, jnp.int32),
            pltpu.VMEM((1, channels), jnp.float32),
            pltpu.VMEM(w_qkv.shape, jnp.bfloat16),
            pltpu.VMEM((12, rows, packed), jnp.bfloat16),
            pltpu.VMEM((keys, chunks * LANES), jnp.bfloat16),
            pltpu.VMEM((chunks, queries, LANES), jnp.float32),
            pltpu.VMEM((chunks, keys, LANES), jnp.float32),
            pltpu.VMEM((chunks, keys, LANES), jnp.float32),
            pltpu.VMEM((REACH + 1, 3 * query_frames, wide), jnp.float32),
            pltpu.VMEM((REACH + 1, 1, wide), jnp.float32),
            pltpu.VMEM((chunks, queries, LANES), jnp.float32),
            pltpu.SemaphoreType.DMA((16,)),
        ],
        compiler_params=pltpu.CompilerParams(vmem_limit_bytes=60 * 1024 * 1024),
        name="window_attention",
    )(*parts, offsets, numerators, norm_gain.reshape(1, channels), w_qkv)


def group_mean(sums, spread, count):
    high = sums.astype(jnp.bfloat16)
    left = sums - high.astype(jnp.float32)
    mid = left.astype(jnp.bfloat16)
    low = (left - mid.astype(jnp.float32)).astype(jnp.bfloat16)
    dot = functools.partial(jnp.dot, preferred_element_type=jnp.float32)
    return (dot(high, spread) + dot(mid, spread) + dot(low, spread)) * (1.0 / count)


def group_act(rows, gain, spread, count):
    sums = sum(jnp.sum(row, axis=1) for row in rows)
    average = group_mean(sums, spread, count)
    cens = [row - average[:, None, :] for row in rows]
    variance = group_mean(sum(jnp.sum(cen * cen, axis=1) for cen in cens), spread, count)
    scale = lax.rsqrt(variance + EPS) * gain
    acts = []
    for cen in cens:
        v = cen * scale[:, None, :]
        acts.append(v / (1.0 + jnp.exp(-v)))
    return acts


def conv_rows(acts, w_ref, taps_ref):
    frames, cols, channels = acts[0].shape
    deep = w_ref.shape[1]
    count = len(acts)
    col = lax.broadcasted_iota(jnp.int32, (frames * cols, 1), 0) % cols
    for r, act in enumerate(acts):
        flat = act.reshape(frames * cols, channels)
        before = jnp.where(col == 0, 0.0, pltpu.roll(flat, 1, 0))
        after = jnp.where(col == cols - 1, 0.0, pltpu.roll(flat, frames * cols - 1, 0))
        for kw, part in enumerate((before, flat, after)):
            start = (3 * r + kw) * deep
            taps_ref[:, start : start + channels] = part.astype(jnp.bfloat16)
    outs = []
    for r in range(count):
        lo, hi = max(r - 1, 0), min(r + 1, count - 1)
        left = taps_ref[:, 3 * lo * deep : 3 * (hi + 1) * deep]
        right = w_ref[3 * (lo - r + 1) : 3 * (hi - r + 2)]
        right = right.reshape(-1, channels)
        out = jnp.dot(left, right, preferred_element_type=jnp.float32)
        outs.append(out.reshape(frames, cols, channels))
    return outs


def res_kernel(*refs):
    sources, out_ref = refs[:10], refs[10]
    (
        part_ref, lat_ref, w_out_ref, gn_ref, step_ref, one_ref, two_ref, comb_ref, taps_ref, sem,
    ) = refs[11:]
    frames, count, cols, channels = lat_ref.shape
    deep = one_ref.shape[1]
    targets = [part_ref.at[i] for i in range(4)] + [w_out_ref, lat_ref, gn_ref, step_ref]
    targets += [ref.at[:, :channels, :] for ref in (one_ref, two_ref)]
    copies = fetch(list(zip(sources, targets)), sem)
    for ref in (one_ref, two_ref):
        ref[:, channels:, :] = jnp.zeros((ref.shape[0], deep - channels, channels), jnp.bfloat16)
    for i in range(3 * count):
        taps_ref[:, i * deep + channels : (i + 1) * deep] = jnp.zeros(
            (frames * cols, deep - channels), jnp.bfloat16
        )
    size = channels // NORM_GROUPS
    group_r = lax.broadcasted_iota(jnp.int32, (channels, channels), 0) // size
    group_c = lax.broadcasted_iota(jnp.int32, (channels, channels), 1) // size
    spread = jnp.where(group_r == group_c, 1.0, 0.0).astype(jnp.bfloat16)
    members = count * cols * size

    core, chip, _ = place()
    half = comb_ref.shape[2] // PACK
    for i, (side, tall) in enumerate(
        ((core, chip), (1 - core, chip), (core, 1 - chip), (1 - core, 1 - chip))
    ):
        copies[i].wait()
        for a, piece in enumerate(unpack_lanes(part_ref[i].astype(jnp.float32))):
            piece = jnp.concatenate(piece, 1)[:, :channels].astype(jnp.bfloat16)
            comb_ref[:, side * 2 + tall, a * half : (a + 1) * half, :] = piece.reshape(
                frames, half, channels
            )
    for copy in copies[4:8]:
        copy.wait()
    combined = comb_ref[...].reshape(frames, count * cols, channels)
    hidden = []
    for r in range(count):
        comb = combined[:, r * cols : (r + 1) * cols, :].reshape(frames * cols, channels)
        proj = jnp.dot(comb, w_out_ref[...], preferred_element_type=jnp.float32)
        hid = lat_ref[:, r].astype(jnp.float32) + proj.reshape(frames, cols, channels)
        hidden.append(hid.astype(jnp.bfloat16).astype(jnp.float32))
    acts = group_act(hidden, gn_ref[0:1], spread, members)
    copies[8].wait()
    middle = [row + step_ref[...][None] for row in conv_rows(acts, one_ref, taps_ref)]
    acts = group_act(middle, gn_ref[1:2], spread, members)
    copies[9].wait()
    for r, row in enumerate(conv_rows(acts, two_ref, taps_ref)):
        out_ref[:, r] = (hidden[r] + row).astype(out_ref.dtype)


def res_block(parts, latents, w_out, gn_gain, conv_one, conv_two, step_embed):
    frames, count, cols, channels = latents.shape
    deep = -(-channels // 128) * 128
    vmem = pl.BlockSpec(memory_space=pltpu.VMEM)
    return pl.pallas_call(
        res_kernel,
        out_shape=jax.ShapeDtypeStruct(latents.shape, jnp.bfloat16),
        in_specs=[pl.BlockSpec(memory_space=pl.ANY)] * 10,
        out_specs=vmem,
        scratch_shapes=[
            pltpu.VMEM((4,) + parts[0].shape, jnp.bfloat16),
            pltpu.VMEM(latents.shape, jnp.bfloat16),
            pltpu.VMEM(w_out.shape, jnp.bfloat16),
            pltpu.VMEM(gn_gain.shape, jnp.float32),
            pltpu.VMEM((1, channels), jnp.float32),
            pltpu.VMEM((9, deep, channels), jnp.bfloat16),
            pltpu.VMEM((9, deep, channels), jnp.bfloat16),
            pltpu.VMEM((frames, QUARTERS, count * cols // QUARTERS, channels), jnp.bfloat16),
            pltpu.VMEM((frames * cols, 3 * count * deep), jnp.bfloat16),
            pltpu.SemaphoreType.DMA((10,)),
        ],
        compiler_params=pltpu.CompilerParams(vmem_limit_bytes=60 * 1024 * 1024),
        name="res_block",
    )(
        *parts,
        w_out,
        latents,
        gn_gain,
        step_embed.reshape(1, channels),
        conv_one.reshape(9, channels, channels),
        conv_two.reshape(9, channels, channels),
    )


def body(
    latents, norm_gain, w_qkv, w_out, gn_gain, conv_one, conv_two, step_embed, offsets, numerators
):
    block_len, tile_rows, tile_cols, channels = latents.shape
    planes = lax.axis_size("frame") // QUARTERS
    cells = tile_rows * tile_cols // QUARTERS
    vmem = pl.BlockSpec(memory_space=pltpu.VMEM)
    rows, packed = block_len * cells // PACK, PACK * channels
    near, far = pl.pallas_call(
        pack_kernel,
        out_shape=[jax.ShapeDtypeStruct((2, rows, packed), jnp.bfloat16)] * 2,
        in_specs=[vmem],
        out_specs=[vmem] * 2,
        name="pack",
    )(latents.reshape(block_len, QUARTERS, cells, channels))
    landed = [
        near,
        moved(far, lambda i: i ^ 2),
        moved(near, lambda i: i + QUARTERS),
        moved(far, lambda i: (i ^ 2) + QUARTERS),
        moved(near, lambda i: i - QUARTERS),
        moved(far, lambda i: (i ^ 2) - QUARTERS),
    ]
    parts = []
    for piece in landed:
        parts += [piece, moved(piece, lambda i: i ^ 1)]
    own, sib, far_own, far_sib = attend(
        parts, norm_gain, w_qkv, offsets, numerators, cells, planes
    )
    pieces = [
        own,
        moved(sib, lambda i: i ^ 1),
        moved(far_own, lambda i: i ^ 2),
        moved(moved(far_sib, lambda i: i ^ 1), lambda i: i ^ 2),
    ]
    return res_block(pieces, latents, w_out, gn_gain, conv_one, conv_two, step_embed)


def solution(mesh):
    return jax.shard_map(
        body,
        mesh=mesh,
        in_specs=(
            P(("groups", "frame"), None, None, None),
            P(),
            P(),
            P(),
            P(),
            P(),
            P(),
            P(),
            P("groups"),
            P(),
        ),
        out_specs=P(("groups", "frame"), None, None, None),
        check_vma=False,
    )
```

```python
import functools

import jax
import jax.numpy as jnp
from jax import lax
from jax.experimental import pallas as pl
from jax.experimental.pallas import tpu as pltpu
from jax.sharding import PartitionSpec as P

HEADS = 5
NORM_GROUPS = 32
BLOCK = 4
WINDOW = 16
REACH = WINDOW // BLOCK
EPS = 1e-05
LANES = 128
GROUP = 2
LOG2E = 1.4426950408889634
NT = (((1,), (1,)), ((), ()))
QUARTERS = 4
PACK = 2


def place():
    me = lax.axis_index("frame")
    return me % 2, me // 2 % 2, me // QUARTERS


def moved(array, target):
    count = lax.axis_size("frame")
    return lax.ppermute(array, "frame", [(i, target(i) % count) for i in range(count)])


def pack_lanes(first, second):
    low = lax.broadcasted_iota(jnp.int32, first[-1].shape, first[-1].ndim - 1) < LANES // 2
    tail = jnp.where(low, first[-1], pltpu.roll(second[-1], LANES // 2, second[-1].ndim - 1))
    return jnp.concatenate(first[:-1] + second[:-1] + [tail], -1)


def unpack_lanes(rows):
    chunks = [rows[:, i : i + LANES] for i in range(0, rows.shape[1], LANES)]
    full = len(chunks) // 2
    low = lax.broadcasted_iota(jnp.int32, chunks[-1].shape, 1) < LANES // 2
    first = chunks[:full] + [jnp.where(low, chunks[-1], 0.0)]
    second = chunks[full:-1] + [jnp.where(low, pltpu.roll(chunks[-1], LANES // 2, 1), 0.0)]
    return first, second


def fetch(pairs, sem):
    copies = [pltpu.make_async_copy(src, dst, sem.at[i]) for i, (src, dst) in enumerate(pairs)]
    for copy in copies:
        copy.start()
    return copies


def pack_kernel(lat_ref, gain_ref, near_ref, far_ref):
    core, chip, _ = place()
    frames, _, cells, channels = lat_ref.shape
    half = cells // PACK
    width = -(-channels // LANES) * LANES
    for out_ref, tall in ((near_ref, chip), (far_ref, 1 - chip)):
        for i, side in enumerate((core, 1 - core)):
            x = lat_ref[:, side * 2 + tall].astype(jnp.float32)
            cen = x - jnp.mean(x, axis=-1, keepdims=True)
            var = jnp.mean(cen * cen, axis=-1, keepdims=True)
            x = cen * lax.rsqrt(var + EPS) * gain_ref[...].reshape(1, 1, channels)
            x = jnp.concatenate([x, jnp.zeros((frames, cells, width - channels), x.dtype)], -1)
            halves = []
            for a in range(PACK):
                rows = x[:, a * half : (a + 1) * half].reshape(frames * half, width)
                halves.append([rows[:, j : j + LANES] for j in range(0, width, LANES)])
            out_ref[i] = pack_lanes(*halves).astype(out_ref.dtype)


def attend_kernel(cells, planes, *refs):
    sources, refs = refs[:12], refs[12:]
    off_hbm, num_hbm, w_hbm, own_ref, sib_ref, far_own_ref, far_sib_ref = refs[:7]
    (
        off_ref, num_ref, w_ref, part_ref, norm_ref, q_ref, k_ref, v_ref, bias_ref, coef_ref, acc_ref, sem,
    ) = refs[7:]
    core, chip, plane = place()
    channels = w_ref.shape[0]
    head_dim = channels // HEADS
    half = cells // PACK
    part_rows = part_ref.shape[1]
    part_frames = part_rows // half
    key_frames, query_frames = part_frames * 12, part_frames * 4
    key_rows, query_rows = key_frames * half, query_frames * half
    blocks = planes * QUARTERS
    frames = blocks * BLOCK
    group = GROUP
    wide = group * HEADS * query_frames
    chunks, lanes = k_ref.shape[0], k_ref.shape[2]
    copies = fetch(
        [(src.at[i % 2], part_ref.at[i]) for i, src in enumerate(sources)]
        + [(w_hbm, w_ref), (off_hbm, off_ref), (num_hbm, num_ref)],
        sem,
    )

    for i in range(len(sources)):
        copies[i].wait()
        for a, x in enumerate(unpack_lanes(part_ref[i].astype(jnp.float32))):
            start = a * key_rows + i * part_rows
            norm_ref[start : start + part_rows] = jnp.concatenate(x, 1).astype(jnp.bfloat16)
    for copy in copies[len(sources) :]:
        copy.wait()
    pad = jnp.zeros((channels, chunks * lanes - channels), jnp.bfloat16)
    below = jnp.zeros((chunks * lanes - channels, chunks * lanes), jnp.bfloat16)
    for i, (out_ref, rows) in enumerate(((q_ref, query_rows), (k_ref, key_rows), (v_ref, key_rows))):
        w = jnp.concatenate([w_ref[:, i * channels : (i + 1) * channels], pad], 1)
        w = jnp.concatenate([w, below], 0)
        for a in range(PACK):
            here = norm_ref[a * key_rows : a * key_rows + rows]
            res = jnp.dot(here, w, preferred_element_type=jnp.float32)
            for j in range(chunks):
                out_ref[j, a * rows : (a + 1) * rows] = res[:, j * lanes : (j + 1) * lanes]

    ids = []
    for step in (0, planes - 1, 1):
        for tall in (chip, 1 - chip):
            base = lax.rem(plane + step, planes) * QUARTERS + 2 * tall
            ids += [base + core, base + 1 - core]
    lane = lax.broadcasted_iota(jnp.int32, (1, wide), 1)
    query = lane % query_frames
    block = jnp.zeros((1, wide), jnp.int32)
    for i in range(query_frames // BLOCK):
        block = jnp.where(query // BLOCK == i, ids[i], block)
    rest = query % BLOCK
    spot = lax.broadcasted_iota(jnp.int32, (key_frames, wide), 0)
    key = jnp.zeros((key_frames, wide), jnp.int32)
    for i, at in enumerate(ids):
        key = jnp.where(spot // BLOCK == i, at * BLOCK, key)
    key = key + spot % BLOCK
    weights = []
    for back in range(REACH + 1):
        owner = block - back
        owner = jnp.where(owner < 0, owner + blocks, owner)
        shift = jnp.zeros((1, wide), jnp.int32)
        for w in range(blocks):
            shift = jnp.where(owner == w, off_ref[w], shift)
        at = BLOCK * back + rest - shift
        weight = jnp.zeros((1, wide), jnp.int32)
        for j in range(WINDOW):
            weight = jnp.where(at == j, num_ref[j], weight)
        weights.append(weight.astype(jnp.float32))
        rel = key - (BLOCK * owner + shift)
        rel = jnp.where(rel < 0, rel + frames, rel)
        bias_ref[back] = jnp.where(rel < WINDOW, 0.0, -1e30)
    total = sum(weights)
    for back in range(REACH + 1):
        coef_ref[back] = weights[back] / total

    lane_head = lax.broadcasted_iota(jnp.int32, (1, chunks * lanes), 1) // head_dim
    lane_cell = lane // (HEADS * query_frames)
    span = HEADS * query_frames

    def rows_of(ref, start, size):
        rows = pl.ds(start, size, stride=half)
        return jnp.concatenate([ref[j, rows, :] for j in range(chunks)], 1)

    def group_step(a, first):
        keys, values, queries = [], [], []
        for g in range(group):
            at = first + g
            keys.append(rows_of(k_ref, a * key_rows + at, key_frames).astype(jnp.bfloat16))
            values.append(rows_of(v_ref, a * key_rows + at, key_frames).astype(jnp.bfloat16))
            q = rows_of(q_ref, a * query_rows + at, query_frames) * (head_dim**-0.5)
            queries += [jnp.where(lane_head == h, q, 0.0) for h in range(HEADS)]
        keys = jnp.concatenate(keys, 0)
        queries = jnp.concatenate(queries, 0).astype(jnp.bfloat16)
        cross = lax.dot_general(keys, queries, NT, preferred_element_type=jnp.float32)
        scores = cross[:key_frames]
        for g in range(1, group):
            scores = jnp.where(lane_cell == g, cross[g * key_frames : (g + 1) * key_frames], scores)
        scores = scores * LOG2E
        mixed = jnp.zeros((key_frames, wide), jnp.float32)
        for back in range(REACH + 1):
            s = scores + bias_ref[back]
            e = jnp.exp2(s - jnp.max(s, axis=0, keepdims=True))
            z = jnp.sum(e, axis=0, keepdims=True)
            mixed = mixed + e * (coef_ref[back] / z)
        mixed = mixed.T.astype(jnp.bfloat16)
        for g in range(group):
            full = jnp.dot(
                mixed[g * span : (g + 1) * span], values[g], preferred_element_type=jnp.float32
            )
            out = full[:query_frames]
            for h in range(1, HEADS):
                out = jnp.where(lane_head == h, full[h * query_frames : (h + 1) * query_frames], out)
            rows = pl.ds(a * query_rows + first + g, query_frames, stride=half)
            for j in range(chunks):
                acc_ref[j, rows, :] = out[:, j * lanes : (j + 1) * lanes]

    for a in range(PACK):
        for first in range(0, half, group):
            group_step(a, first)
    quarter = query_rows // 4
    for i, out_ref in enumerate((own_ref, sib_ref, far_own_ref, far_sib_ref)):
        pieces = []
        for a in range(PACK):
            start = a * query_rows + i * quarter
            pieces.append([acc_ref[j, start : start + quarter] for j in range(chunks)])
        out_ref[...] = pack_lanes(*pieces).astype(out_ref.dtype)


def attend(parts, w_qkv, offsets, numerators, cells, planes):
    channels = w_qkv.shape[0]
    vmem = pl.BlockSpec(memory_space=pltpu.VMEM)
    _, rows, packed = parts[0].shape
    chunks = -(-channels // LANES)
    query_frames = 4 * rows * PACK // cells
    wide = GROUP * HEADS * query_frames
    keys, queries = 12 * rows * PACK, 4 * rows * PACK
    return pl.pallas_call(
        functools.partial(attend_kernel, cells, planes),
        out_shape=[jax.ShapeDtypeStruct((rows, packed), jnp.bfloat16)] * 4,
        in_specs=[pl.BlockSpec(memory_space=pl.ANY)] * 15,
        out_specs=[vmem] * 4,
        scratch_shapes=[
            pltpu.SMEM(offsets.shape, jnp.int32),
            pltpu.SMEM(numerators.shape, jnp.int32),
            pltpu.VMEM(w_qkv.shape, jnp.bfloat16),
            pltpu.VMEM((12, rows, packed), jnp.bfloat16),
            pltpu.VMEM((keys, chunks * LANES), jnp.bfloat16),
            pltpu.VMEM((chunks, queries, LANES), jnp.float32),
            pltpu.VMEM((chunks, keys, LANES), jnp.float32),
            pltpu.VMEM((chunks, keys, LANES), jnp.float32),
            pltpu.VMEM((REACH + 1, 3 * query_frames, wide), jnp.float32),
            pltpu.VMEM((REACH + 1, 1, wide), jnp.float32),
            pltpu.VMEM((chunks, queries, LANES), jnp.float32),
            pltpu.SemaphoreType.DMA((15,)),
        ],
        compiler_params=pltpu.CompilerParams(vmem_limit_bytes=60 * 1024 * 1024),
        name="window_attention",
    )(*parts, offsets, numerators, w_qkv)


def group_mean(sums, spread, count):
    high = sums.astype(jnp.bfloat16)
    left = sums - high.astype(jnp.float32)
    mid = left.astype(jnp.bfloat16)
    low = (left - mid.astype(jnp.float32)).astype(jnp.bfloat16)
    dot = functools.partial(jnp.dot, preferred_element_type=jnp.float32)
    return (dot(high, spread) + dot(mid, spread) + dot(low, spread)) * (1.0 / count)


def group_act(rows, gain, spread, count):
    sums = sum(jnp.sum(row, axis=1) for row in rows)
    average = group_mean(sums, spread, count)
    cens = [row - average[:, None, :] for row in rows]
    variance = group_mean(sum(jnp.sum(cen * cen, axis=1) for cen in cens), spread, count)
    scale = lax.rsqrt(variance + EPS) * gain
    acts = []
    for cen in cens:
        v = cen * scale[:, None, :]
        acts.append(v / (1.0 + jnp.exp(-v)))
    return acts


def conv_rows(acts, w_ref, taps_ref):
    frames, cols, channels = acts[0].shape
    deep = w_ref.shape[1]
    count = len(acts)
    col = lax.broadcasted_iota(jnp.int32, (frames * cols, 1), 0) % cols
    for r, act in enumerate(acts):
        flat = act.reshape(frames * cols, channels)
        before = jnp.where(col == 0, 0.0, pltpu.roll(flat, 1, 0))
        after = jnp.where(col == cols - 1, 0.0, pltpu.roll(flat, frames * cols - 1, 0))
        for kw, part in enumerate((before, flat, after)):
            start = (3 * r + kw) * deep
            taps_ref[:, start : start + channels] = part.astype(jnp.bfloat16)
    outs = []
    for r in range(count):
        lo, hi = max(r - 1, 0), min(r + 1, count - 1)
        left = taps_ref[:, 3 * lo * deep : 3 * (hi + 1) * deep]
        right = w_ref[3 * (lo - r + 1) : 3 * (hi - r + 2)]
        right = right.reshape(-1, channels)
        out = jnp.dot(left, right, preferred_element_type=jnp.float32)
        outs.append(out.reshape(frames, cols, channels))
    return outs


def res_kernel(*refs):
    sources, out_ref = refs[:10], refs[10]
    (
        part_ref, lat_ref, w_out_ref, gn_ref, step_ref, one_ref, two_ref, comb_ref, taps_ref, sem,
    ) = refs[11:]
    frames, count, cols, channels = lat_ref.shape
    deep = one_ref.shape[1]
    targets = [part_ref.at[i] for i in range(4)] + [w_out_ref, lat_ref, gn_ref, step_ref]
    targets += [ref.at[:, :channels, :] for ref in (one_ref, two_ref)]
    copies = fetch(list(zip(sources, targets)), sem)
    for ref in (one_ref, two_ref):
        ref[:, channels:, :] = jnp.zeros((ref.shape[0], deep - channels, channels), jnp.bfloat16)
    for i in range(3 * count):
        taps_ref[:, i * deep + channels : (i + 1) * deep] = jnp.zeros(
            (frames * cols, deep - channels), jnp.bfloat16
        )
    size = channels // NORM_GROUPS
    group_r = lax.broadcasted_iota(jnp.int32, (channels, channels), 0) // size
    group_c = lax.broadcasted_iota(jnp.int32, (channels, channels), 1) // size
    spread = jnp.where(group_r == group_c, 1.0, 0.0).astype(jnp.bfloat16)
    members = count * cols * size

    core, chip, _ = place()
    half = comb_ref.shape[2] // PACK
    for i, (side, tall) in enumerate(
        ((core, chip), (1 - core, chip), (core, 1 - chip), (1 - core, 1 - chip))
    ):
        copies[i].wait()
        for a, piece in enumerate(unpack_lanes(part_ref[i].astype(jnp.float32))):
            piece = jnp.concatenate(piece, 1)[:, :channels].astype(jnp.bfloat16)
            comb_ref[:, side * 2 + tall, a * half : (a + 1) * half, :] = piece.reshape(
                frames, half, channels
            )
    for copy in copies[4:8]:
        copy.wait()
    combined = comb_ref[...].reshape(frames, count * cols, channels)
    hidden = []
    for r in range(count):
        comb = combined[:, r * cols : (r + 1) * cols, :].reshape(frames * cols, channels)
        proj = jnp.dot(comb, w_out_ref[...], preferred_element_type=jnp.float32)
        hid = lat_ref[:, r].astype(jnp.float32) + proj.reshape(frames, cols, channels)
        hidden.append(hid.astype(jnp.bfloat16).astype(jnp.float32))
    acts = group_act(hidden, gn_ref[0:1], spread, members)
    copies[8].wait()
    middle = [row + step_ref[...].reshape(1, 1, channels) for row in conv_rows(acts, one_ref, taps_ref)]
    acts = group_act(middle, gn_ref[1:2], spread, members)
    copies[9].wait()
    for r, row in enumerate(conv_rows(acts, two_ref, taps_ref)):
        out_ref[:, r] = (hidden[r] + row).astype(out_ref.dtype)


def res_block(parts, latents, w_out, gn_gain, conv_one, conv_two, step_embed):
    frames, count, cols, channels = latents.shape
    deep = -(-channels // 128) * 128
    vmem = pl.BlockSpec(memory_space=pltpu.VMEM)
    return pl.pallas_call(
        res_kernel,
        out_shape=jax.ShapeDtypeStruct(latents.shape, jnp.bfloat16),
        in_specs=[pl.BlockSpec(memory_space=pl.ANY)] * 10,
        out_specs=vmem,
        scratch_shapes=[
            pltpu.VMEM((4,) + parts[0].shape, jnp.bfloat16),
            pltpu.VMEM(latents.shape, jnp.bfloat16),
            pltpu.VMEM(w_out.shape, jnp.bfloat16),
            pltpu.VMEM(gn_gain.shape, jnp.float32),
            pltpu.VMEM(step_embed.shape, jnp.float32),
            pltpu.VMEM((9, deep, channels), jnp.bfloat16),
            pltpu.VMEM((9, deep, channels), jnp.bfloat16),
            pltpu.VMEM((frames, QUARTERS, count * cols // QUARTERS, channels), jnp.bfloat16),
            pltpu.VMEM((frames * cols, 3 * count * deep), jnp.bfloat16),
            pltpu.SemaphoreType.DMA((10,)),
        ],
        compiler_params=pltpu.CompilerParams(vmem_limit_bytes=60 * 1024 * 1024),
        name="res_block",
    )(
        *parts,
        w_out,
        latents,
        gn_gain,
        step_embed,
        conv_one.reshape(9, channels, channels),
        conv_two.reshape(9, channels, channels),
    )


def body(
    latents, norm_gain, w_qkv, w_out, gn_gain, conv_one, conv_two, step_embed, offsets, numerators
):
    block_len, tile_rows, tile_cols, channels = latents.shape
    planes = lax.axis_size("frame") // QUARTERS
    cells = tile_rows * tile_cols // QUARTERS
    vmem = pl.BlockSpec(memory_space=pltpu.VMEM)
    rows, packed = block_len * cells // PACK, PACK * channels
    near, far = pl.pallas_call(
        pack_kernel,
        out_shape=[jax.ShapeDtypeStruct((2, rows, packed), jnp.bfloat16)] * 2,
        in_specs=[vmem] * 2,
        out_specs=[vmem] * 2,
        name="norm_pack",
    )(latents.reshape(block_len, QUARTERS, cells, channels), norm_gain)
    landed = [
        near,
        moved(far, lambda i: i ^ 2),
        moved(near, lambda i: i + QUARTERS),
        moved(far, lambda i: (i ^ 2) + QUARTERS),
        moved(near, lambda i: i - QUARTERS),
        moved(far, lambda i: (i ^ 2) - QUARTERS),
    ]
    landed[:4] = lax.optimization_barrier(landed[:4])
    parts = []
    for piece in landed:
        parts += [piece, moved(piece, lambda i: i ^ 1)]
    own, sib, far_own, far_sib = attend(
        parts, w_qkv, offsets, numerators, cells, planes
    )
    pieces = [
        own,
        moved(sib, lambda i: i ^ 1),
        moved(far_own, lambda i: i ^ 2),
        moved(far_sib, lambda i: i ^ 3),
    ]
    return res_block(pieces, latents, w_out, gn_gain, conv_one, conv_two, step_embed)


def solution(mesh):
    return jax.shard_map(
        body,
        mesh=mesh,
        in_specs=(
            P(("groups", "frame"), None, None, None),
            P(),
            P(),
            P(),
            P(),
            P(),
            P(),
            P(),
            P("groups"),
            P(),
        ),
        out_specs=P(("groups", "frame"), None, None, None),
        check_vma=False,
    )
```

```python
import functools

import jax
import jax.numpy as jnp
from jax import lax
from jax.experimental import pallas as pl
from jax.experimental.pallas import tpu as pltpu
from jax.sharding import PartitionSpec as P

HEADS = 5
NORM_GROUPS = 32
BLOCK = 4
WINDOW = 16
REACH = WINDOW // BLOCK
EPS = 1e-05
LANES = 128
GROUP = 2
LOG2E = 1.4426950408889634
NT = (((1,), (1,)), ((), ()))
QUARTERS = 4
PACK = 2


def place():
    me = lax.axis_index("frame")
    return me % 2, me // 2 % 2, me // QUARTERS


def moved(array, target):
    count = lax.axis_size("frame")
    return lax.ppermute(array, "frame", [(i, target(i) % count) for i in range(count)])


def pack_lanes(first, second):
    low = lax.broadcasted_iota(jnp.int32, first[-1].shape, first[-1].ndim - 1) < LANES // 2
    tail = jnp.where(low, first[-1], pltpu.roll(second[-1], LANES // 2, second[-1].ndim - 1))
    return jnp.concatenate(first[:-1] + second[:-1] + [tail], -1)


def unpack_lanes(rows):
    chunks = [rows[:, i : i + LANES] for i in range(0, rows.shape[1], LANES)]
    full = len(chunks) // 2
    low = lax.broadcasted_iota(jnp.int32, chunks[-1].shape, 1) < LANES // 2
    first = chunks[:full] + [jnp.where(low, chunks[-1], 0.0)]
    second = chunks[full:-1] + [jnp.where(low, pltpu.roll(chunks[-1], LANES // 2, 1), 0.0)]
    return first, second


def fetch(pairs, sem):
    copies = [pltpu.make_async_copy(src, dst, sem.at[i]) for i, (src, dst) in enumerate(pairs)]
    for copy in copies:
        copy.start()
    return copies


def pack_kernel(lat_ref, gain_ref, near_ref, far_ref):
    core, chip, _ = place()
    frames, _, cells, channels = lat_ref.shape
    half = cells // PACK
    width = -(-channels // LANES) * LANES
    for out_ref, tall in ((near_ref, chip), (far_ref, 1 - chip)):
        for i, side in enumerate((core, 1 - core)):
            x = lat_ref[:, side * 2 + tall].astype(jnp.float32)
            cen = x - jnp.mean(x, axis=-1, keepdims=True)
            var = jnp.mean(cen * cen, axis=-1, keepdims=True)
            x = cen * lax.rsqrt(var + EPS) * gain_ref[...].reshape(1, 1, channels)
            x = jnp.concatenate([x, jnp.zeros((frames, cells, width - channels), x.dtype)], -1)
            halves = []
            for a in range(PACK):
                rows = x[:, a * half : (a + 1) * half].reshape(frames * half, width)
                halves.append([rows[:, j : j + LANES] for j in range(0, width, LANES)])
            out_ref[i] = pack_lanes(*halves).astype(out_ref.dtype)


def attend_kernel(cells, planes, *refs):
    sources, refs = refs[:12], refs[12:]
    ints_hbm, w_ref, own_ref, sib_ref, far_own_ref, far_sib_ref = refs[:6]
    (
        ints_ref, part_ref, norm_ref, q_ref, k_ref, v_ref, bias_ref, coef_ref, acc_ref, sem,
    ) = refs[6:]
    core, chip, plane = place()
    channels = own_ref.shape[1] // PACK
    head_dim = channels // HEADS
    half = cells // PACK
    part_rows = part_ref.shape[1]
    part_frames = part_rows // half
    key_frames, query_frames = part_frames * 12, part_frames * 4
    key_rows, query_rows = key_frames * half, query_frames * half
    blocks = planes * QUARTERS
    frames = blocks * BLOCK
    group = GROUP
    wide = group * HEADS * query_frames
    chunks, lanes = k_ref.shape[0], k_ref.shape[2]
    copies = fetch(
        [(src.at[i % 2], part_ref.at[i]) for i, src in enumerate(sources)]
        + [(ints_hbm, ints_ref)],
        sem,
    )

    for i in range(len(sources)):
        copies[i].wait()
        for a, x in enumerate(unpack_lanes(part_ref[i].astype(jnp.float32))):
            start = a * key_rows + i * part_rows
            norm_ref[start : start + part_rows] = jnp.concatenate(x, 1).astype(jnp.bfloat16)
    for copy in copies[len(sources) :]:
        copy.wait()
    pad = jnp.zeros((chunks * lanes, chunks * lanes - channels), jnp.bfloat16)
    for i, (out_ref, rows) in enumerate(((q_ref, query_rows), (k_ref, key_rows), (v_ref, key_rows))):
        w = jnp.concatenate([w_ref[:, i * channels : (i + 1) * channels], pad], 1)
        for a in range(PACK):
            here = norm_ref[a * key_rows : a * key_rows + rows]
            res = jnp.dot(here, w, preferred_element_type=jnp.float32)
            for j in range(chunks):
                out_ref[j, a * rows : (a + 1) * rows] = res[:, j * lanes : (j + 1) * lanes]

    ids = []
    for step in (0, planes - 1, 1):
        for tall in (chip, 1 - chip):
            base = lax.rem(plane + step, planes) * QUARTERS + 2 * tall
            ids += [base + core, base + 1 - core]
    lane = lax.broadcasted_iota(jnp.int32, (1, wide), 1)
    query = lane % query_frames
    block = jnp.zeros((1, wide), jnp.int32)
    for i in range(query_frames // BLOCK):
        block = jnp.where(query // BLOCK == i, ids[i], block)
    rest = query % BLOCK
    spot = lax.broadcasted_iota(jnp.int32, (key_frames, wide), 0)
    key = jnp.zeros((key_frames, wide), jnp.int32)
    for i, at in enumerate(ids):
        key = jnp.where(spot // BLOCK == i, at * BLOCK, key)
    key = key + spot % BLOCK
    weights = []
    for back in range(REACH + 1):
        owner = block - back
        owner = jnp.where(owner < 0, owner + blocks, owner)
        shift = jnp.zeros((1, wide), jnp.int32)
        for w in range(blocks):
            shift = jnp.where(owner == w, ints_ref[w], shift)
        at = BLOCK * back + rest - shift
        weight = jnp.zeros((1, wide), jnp.int32)
        for j in range(WINDOW):
            weight = jnp.where(at == j, ints_ref[blocks + j], weight)
        weights.append(weight.astype(jnp.float32))
        rel = key - (BLOCK * owner + shift)
        rel = jnp.where(rel < 0, rel + frames, rel)
        bias_ref[back] = jnp.where(rel < WINDOW, 0.0, -1e30)
    total = sum(weights)
    for back in range(REACH + 1):
        coef_ref[back] = weights[back] / total

    lane_head = lax.broadcasted_iota(jnp.int32, (1, chunks * lanes), 1) // head_dim
    lane_cell = lane // (HEADS * query_frames)
    span = HEADS * query_frames

    def rows_of(ref, start, size):
        rows = pl.ds(start, size, stride=half)
        return jnp.concatenate([ref[j, rows, :] for j in range(chunks)], 1)

    def group_step(a, first):
        keys, values, queries = [], [], []
        for g in range(group):
            at = first + g
            keys.append(rows_of(k_ref, a * key_rows + at, key_frames).astype(jnp.bfloat16))
            values.append(rows_of(v_ref, a * key_rows + at, key_frames).astype(jnp.bfloat16))
            q = rows_of(q_ref, a * query_rows + at, query_frames) * (head_dim**-0.5)
            queries += [jnp.where(lane_head == h, q, 0.0) for h in range(HEADS)]
        keys = jnp.concatenate(keys, 0)
        queries = jnp.concatenate(queries, 0).astype(jnp.bfloat16)
        cross = lax.dot_general(keys, queries, NT, preferred_element_type=jnp.float32)
        scores = cross[:key_frames]
        for g in range(1, group):
            scores = jnp.where(lane_cell == g, cross[g * key_frames : (g + 1) * key_frames], scores)
        scores = scores * LOG2E
        mixed = jnp.zeros((key_frames, wide), jnp.float32)
        for back in range(REACH + 1):
            s = scores + bias_ref[back]
            e = jnp.exp2(s - jnp.max(s, axis=0, keepdims=True))
            z = jnp.sum(e, axis=0, keepdims=True)
            mixed = mixed + e * (coef_ref[back] / z)
        mixed = mixed.T.astype(jnp.bfloat16)
        for g in range(group):
            full = jnp.dot(
                mixed[g * span : (g + 1) * span], values[g], preferred_element_type=jnp.float32
            )
            out = full[:query_frames]
            for h in range(1, HEADS):
                out = jnp.where(lane_head == h, full[h * query_frames : (h + 1) * query_frames], out)
            rows = pl.ds(a * query_rows + first + g, query_frames, stride=half)
            for j in range(chunks):
                acc_ref[j, rows, :] = out[:, j * lanes : (j + 1) * lanes]

    for a in range(PACK):
        for first in range(0, half, group):
            group_step(a, first)
    quarter = query_rows // 4
    for i, out_ref in enumerate((own_ref, sib_ref, far_own_ref, far_sib_ref)):
        pieces = []
        for a in range(PACK):
            start = a * query_rows + i * quarter
            pieces.append([acc_ref[j, start : start + quarter] for j in range(chunks)])
        out_ref[...] = pack_lanes(*pieces).astype(out_ref.dtype)


def attend(parts, w_wide, ints, cells, planes):
    channels = w_wide.shape[1] // 3
    vmem = pl.BlockSpec(memory_space=pltpu.VMEM)
    _, rows, packed = parts[1].shape
    chunks = -(-channels // LANES)
    query_frames = 4 * rows * PACK // cells
    wide = GROUP * HEADS * query_frames
    keys, queries = 12 * rows * PACK, 4 * rows * PACK
    return pl.pallas_call(
        functools.partial(attend_kernel, cells, planes),
        out_shape=[jax.ShapeDtypeStruct((rows, packed), jnp.bfloat16)] * 4,
        in_specs=[pl.BlockSpec(memory_space=pl.ANY)] * 13 + [vmem],
        out_specs=[vmem] * 4,
        scratch_shapes=[
            pltpu.SMEM(ints.shape, jnp.int32),
            pltpu.VMEM((12, rows, packed), jnp.bfloat16),
            pltpu.VMEM((keys, chunks * LANES), jnp.bfloat16),
            pltpu.VMEM((chunks, queries, LANES), jnp.float32),
            pltpu.VMEM((chunks, keys, LANES), jnp.float32),
            pltpu.VMEM((chunks, keys, LANES), jnp.float32),
            pltpu.VMEM((REACH + 1, 3 * query_frames, wide), jnp.float32),
            pltpu.VMEM((REACH + 1, 1, wide), jnp.float32),
            pltpu.VMEM((chunks, queries, LANES), jnp.float32),
            pltpu.SemaphoreType.DMA((13,)),
        ],
        compiler_params=pltpu.CompilerParams(vmem_limit_bytes=30 * 1024 * 1024),
        name="window_attention",
    )(*parts, ints, w_wide)


def group_mean(sums, spread, count):
    high = sums.astype(jnp.bfloat16)
    left = sums - high.astype(jnp.float32)
    mid = left.astype(jnp.bfloat16)
    low = (left - mid.astype(jnp.float32)).astype(jnp.bfloat16)
    dot = functools.partial(jnp.dot, preferred_element_type=jnp.float32)
    return (dot(high, spread) + dot(mid, spread) + dot(low, spread)) * (1.0 / count)


def group_act(rows, gain, spread, count):
    sums = sum(jnp.sum(row, axis=1) for row in rows)
    average = group_mean(sums, spread, count)
    cens = [row - average[:, None, :] for row in rows]
    variance = group_mean(sum(jnp.sum(cen * cen, axis=1) for cen in cens), spread, count)
    scale = lax.rsqrt(variance + EPS) * gain
    acts = []
    for cen in cens:
        v = cen * scale[:, None, :]
        acts.append(v / (1.0 + jnp.exp(-v)))
    return acts


def conv_rows(acts, w_ref, taps_ref):
    frames, cols, channels = acts[0].shape
    deep = w_ref.shape[2]
    count = len(acts)
    col = lax.broadcasted_iota(jnp.int32, (frames * cols, 1), 0) % cols
    for r, act in enumerate(acts):
        flat = act.reshape(frames * cols, channels)
        before = jnp.where(col == 0, 0.0, pltpu.roll(flat, 1, 0))
        after = jnp.where(col == cols - 1, 0.0, pltpu.roll(flat, frames * cols - 1, 0))
        for kw, part in enumerate((before, flat, after)):
            start = (3 * r + kw) * deep
            taps_ref[:, start : start + channels] = part.astype(jnp.bfloat16)
    outs = []
    for r in range(count):
        lo, hi = max(r - 1, 0), min(r + 1, count - 1)
        left = taps_ref[:, 3 * lo * deep : 3 * (hi + 1) * deep]
        right = w_ref[lo - r + 1 : hi - r + 2]
        right = right.reshape(-1, channels)
        out = jnp.dot(left, right, preferred_element_type=jnp.float32)
        outs.append(out.reshape(frames, cols, channels))
    return outs


def res_kernel(*refs):
    part_refs, (lat_ref, w_out_ref, gn_ref, one_ref, two_ref, out_ref) = refs[:4], refs[4:10]
    comb_ref, taps_ref = refs[10:]
    count, frames, cols, channels = lat_ref.shape
    deep = one_ref.shape[2]
    for i in range(3 * count):
        taps_ref[:, i * deep + channels : (i + 1) * deep] = jnp.zeros(
            (frames * cols, deep - channels), jnp.bfloat16
        )
    size = channels // NORM_GROUPS
    group_r = lax.broadcasted_iota(jnp.int32, (channels, 1), 0) // size
    group_c = lax.broadcasted_iota(jnp.int32, (1, channels), 1) // size
    spread = jnp.where(group_r == group_c, 1.0, 0.0).astype(jnp.bfloat16)
    members = count * cols * size

    core, chip, _ = place()
    half = comb_ref.shape[2] // PACK
    for i, (side, tall) in enumerate(
        ((core, chip), (1 - core, chip), (core, 1 - chip), (1 - core, 1 - chip))
    ):
        for a, piece in enumerate(unpack_lanes(part_refs[i][...].astype(jnp.float32))):
            piece = jnp.concatenate(piece, 1)[:, :channels].astype(jnp.bfloat16)
            comb_ref[:, side * 2 + tall, a * half : (a + 1) * half, :] = piece.reshape(
                frames, half, channels
            )
    combined = comb_ref[...].reshape(frames, count * cols, channels)
    hidden = []
    for r in range(count):
        comb = combined[:, r * cols : (r + 1) * cols, :].reshape(frames * cols, channels)
        proj = jnp.dot(comb, w_out_ref[:channels], preferred_element_type=jnp.float32)
        hid = lat_ref[r].astype(jnp.float32) + proj.reshape(frames, cols, channels)
        hidden.append(hid.astype(jnp.bfloat16).astype(jnp.float32))
    acts = group_act(hidden, gn_ref[0:1], spread, members)
    middle = [row + gn_ref[2:3][None] for row in conv_rows(acts, one_ref, taps_ref)]
    acts = group_act(middle, gn_ref[1:2], spread, members)
    for r, row in enumerate(conv_rows(acts, two_ref, taps_ref)):
        out_ref[:, r] = (hidden[r] + row).astype(out_ref.dtype)


def res_block(parts, extras):
    count, frames, cols, channels = extras[0].shape
    deep = -(-channels // LANES) * LANES
    vmem = pl.BlockSpec(memory_space=pltpu.VMEM)
    return pl.pallas_call(
        res_kernel,
        out_shape=jax.ShapeDtypeStruct((frames, count, cols, channels), jnp.bfloat16),
        in_specs=[vmem] * 9,
        out_specs=vmem,
        scratch_shapes=[
            pltpu.VMEM((frames, QUARTERS, count * cols // QUARTERS, channels), jnp.bfloat16),
            pltpu.VMEM((frames * cols, 3 * count * deep), jnp.bfloat16),
        ],
        compiler_params=pltpu.CompilerParams(vmem_limit_bytes=30 * 1024 * 1024),
        name="res_block",
    )(
        *parts,
        *extras,
    )


def body(
    latents, norm_gain, w_qkv, w_out, gn_gain, conv_one, conv_two, step_embed, offsets, numerators
):
    block_len, tile_rows, tile_cols, channels = latents.shape
    planes = lax.axis_size("frame") // QUARTERS
    cells = tile_rows * tile_cols // QUARTERS
    vmem = pl.BlockSpec(memory_space=pltpu.VMEM)
    rows, packed = block_len * cells // PACK, PACK * channels
    near, far = pl.pallas_call(
        pack_kernel,
        out_shape=[jax.ShapeDtypeStruct((2, rows, packed), jnp.bfloat16)] * 2,
        in_specs=[vmem] * 2,
        out_specs=[vmem] * 2,
        name="norm_pack",
    )(latents.reshape(block_len, QUARTERS, cells, channels), norm_gain)
    landed = [
        near,
        moved(far, lambda i: i ^ 2),
        moved(near, lambda i: i + QUARTERS),
        moved(far, lambda i: (i ^ 2) + QUARTERS),
        moved(near, lambda i: i - QUARTERS),
        moved(far, lambda i: (i ^ 2) - QUARTERS),
    ]
    more = (0, -channels % LANES)
    extras = [
        jnp.pad(w_qkv, (more, (0, 0))),
        jnp.concatenate([offsets, numerators]),
        latents.transpose(1, 0, 2, 3),
        jnp.pad(w_out, (more, (0, 0))),
        jnp.concatenate([gn_gain, step_embed[None]]),
        jnp.pad(conv_one, ((0, 0), (0, 0), more, (0, 0))),
        jnp.pad(conv_two, ((0, 0), (0, 0), more, (0, 0))),
    ]
    landed[1:4] = lax.optimization_barrier(landed[1:4])
    landed[0], extras = lax.optimization_barrier((near, extras))
    parts = []
    for piece in landed:
        parts += [piece, moved(piece, lambda i: i ^ 1)]
    parts[0] = parts[0][:1]
    w_wide, ints, *extras = extras
    own, sib, far_own, far_sib = attend(parts, w_wide, ints, cells, planes)
    pieces = [
        own,
        moved(sib, lambda i: i ^ 1),
        moved(far_own, lambda i: i ^ 2),
        moved(far_sib, lambda i: i ^ 3),
    ]
    return res_block(pieces, extras)


def solution(mesh):
    return jax.shard_map(
        body,
        mesh=mesh,
        in_specs=(
            P(("groups", "frame"), None, None, None),
            P(),
            P(),
            P(),
            P(),
            P(),
            P(),
            P(),
            P("groups"),
            P(),
        ),
        out_specs=P(("groups", "frame"), None, None, None),
        check_vma=False,
    )
```

```python
import functools

import jax
import jax.numpy as jnp
from jax import lax
from jax.experimental import pallas as pl
from jax.experimental.pallas import tpu as pltpu
from jax.sharding import PartitionSpec as P

HEADS = 5
NORM_GROUPS = 32
BLOCK = 4
WINDOW = 16
REACH = WINDOW // BLOCK
EPS = 1e-05
LANES = 128
GROUP = 2
LOG2E = 1.4426950408889634
NT = (((1,), (1,)), ((), ()))
QUARTERS = 4
PACK = 2


def place():
    me = lax.axis_index("frame")
    return me % 2, me // 2 % 2, me // QUARTERS


def moved(array, target):
    count = lax.axis_size("frame")
    return lax.ppermute(array, "frame", [(i, target(i) % count) for i in range(count)])


def pack_lanes(first, second):
    low = lax.broadcasted_iota(jnp.int32, first[-1].shape, first[-1].ndim - 1) < LANES // 2
    tail = jnp.where(low, first[-1], pltpu.roll(second[-1], LANES // 2, second[-1].ndim - 1))
    return jnp.concatenate(first[:-1] + second[:-1] + [tail], -1)


def unpack_lanes(rows):
    chunks = [rows[:, i : i + LANES] for i in range(0, rows.shape[1], LANES)]
    full = len(chunks) // 2
    low = lax.broadcasted_iota(jnp.int32, chunks[-1].shape, 1) < LANES // 2
    first = chunks[:full] + [jnp.where(low, chunks[-1], 0.0)]
    second = chunks[full:-1] + [jnp.where(low, pltpu.roll(chunks[-1], LANES // 2, 1), 0.0)]
    return first, second


def pack_kernel(lat_ref, gain_ref, near_ref, far_ref):
    core, chip, _ = place()
    frames, _, cells, channels = lat_ref.shape
    half = cells // PACK
    width = -(-channels // LANES) * LANES
    for out_ref, tall in ((near_ref, chip), (far_ref, 1 - chip)):
        for i, side in enumerate((core, 1 - core)):
            x = lat_ref[:, side * 2 + tall].astype(jnp.float32)
            cen = x - jnp.mean(x, axis=-1, keepdims=True)
            var = jnp.mean(cen * cen, axis=-1, keepdims=True)
            x = cen * lax.rsqrt(var + EPS) * gain_ref[...].reshape(1, 1, channels)
            x = jnp.concatenate([x, jnp.zeros((frames, cells, width - channels), x.dtype)], -1)
            halves = []
            for a in range(PACK):
                rows = x[:, a * half : (a + 1) * half].reshape(frames * half, width)
                halves.append([rows[:, j : j + LANES] for j in range(0, width, LANES)])
            out_ref[i] = pack_lanes(*halves).astype(out_ref.dtype)


def attend_kernel(cells, planes, *refs):
    sources, refs = refs[:12], refs[12:]
    ints_hbm, w_ref, own_ref, sib_ref, far_own_ref, far_sib_ref = refs[:6]
    (
        ints_ref, norm_ref, q_ref, k_ref, v_ref, bias_ref, coef_ref, acc_ref, sem,
    ) = refs[6:]
    core, chip, plane = place()
    channels = own_ref.shape[1] // PACK
    head_dim = channels // HEADS
    half = cells // PACK
    part_rows = sources[1].shape[1]
    part_frames = part_rows // half
    key_frames, query_frames = part_frames * 12, part_frames * 4
    key_rows, query_rows = key_frames * half, query_frames * half
    blocks = planes * QUARTERS
    frames = blocks * BLOCK
    group = GROUP
    wide = group * HEADS * query_frames
    chunks, lanes = k_ref.shape[0], k_ref.shape[2]
    copy = pltpu.make_async_copy(ints_hbm, ints_ref, sem)
    copy.start()

    for i in range(len(sources)):
        for a, x in enumerate(unpack_lanes(sources[i][i % 2].astype(jnp.float32))):
            start = a * key_rows + i * part_rows
            norm_ref[start : start + part_rows] = jnp.concatenate(x, 1).astype(jnp.bfloat16)
    pad = jnp.zeros((chunks * lanes, chunks * lanes - channels), jnp.bfloat16)
    for i, (out_ref, rows) in enumerate(((q_ref, query_rows), (k_ref, key_rows), (v_ref, key_rows))):
        w = jnp.concatenate([w_ref[:, i * channels : (i + 1) * channels], pad], 1)
        for a in range(PACK):
            here = norm_ref[a * key_rows : a * key_rows + rows]
            res = jnp.dot(here, w, preferred_element_type=jnp.float32)
            for j in range(chunks):
                out_ref[j, a * rows : (a + 1) * rows] = res[:, j * lanes : (j + 1) * lanes]

    copy.wait()
    ids = []
    for step in (0, planes - 1, 1):
        for tall in (chip, 1 - chip):
            base = lax.rem(plane + step, planes) * QUARTERS + 2 * tall
            ids += [base + core, base + 1 - core]
    lane = lax.broadcasted_iota(jnp.int32, (1, wide), 1)
    query = lane % query_frames
    block = jnp.zeros((1, wide), jnp.int32)
    for i in range(query_frames // BLOCK):
        block = jnp.where(query // BLOCK == i, ids[i], block)
    rest = query % BLOCK
    spot = lax.broadcasted_iota(jnp.int32, (key_frames, wide), 0)
    key = jnp.zeros((key_frames, wide), jnp.int32)
    for i, at in enumerate(ids):
        key = jnp.where(spot // BLOCK == i, at * BLOCK, key)
    key = key + spot % BLOCK
    weights = []
    for back in range(REACH + 1):
        owner = block - back
        owner = jnp.where(owner < 0, owner + blocks, owner)
        shift = jnp.zeros((1, wide), jnp.int32)
        for w in range(blocks):
            shift = jnp.where(owner == w, ints_ref[w], shift)
        at = BLOCK * back + rest - shift
        weight = jnp.zeros((1, wide), jnp.int32)
        for j in range(WINDOW):
            weight = jnp.where(at == j, ints_ref[blocks + j], weight)
        weights.append(weight.astype(jnp.float32))
        rel = key - (BLOCK * owner + shift)
        rel = jnp.where(rel < 0, rel + frames, rel)
        bias_ref[back] = jnp.where(rel < WINDOW, 0.0, -1e30)
    total = sum(weights)
    for back in range(REACH + 1):
        coef_ref[back] = weights[back] / total

    lane_head = lax.broadcasted_iota(jnp.int32, (1, chunks * lanes), 1) // head_dim
    lane_cell = lane // (HEADS * query_frames)
    span = HEADS * query_frames

    def rows_of(ref, start, size):
        rows = pl.ds(start, size, stride=half)
        return jnp.concatenate([ref[j, rows, :] for j in range(chunks)], 1)

    def group_step(a, first):
        keys, values, queries = [], [], []
        for g in range(group):
            at = first + g
            keys.append(rows_of(k_ref, a * key_rows + at, key_frames).astype(jnp.bfloat16))
            values.append(rows_of(v_ref, a * key_rows + at, key_frames).astype(jnp.bfloat16))
            q = rows_of(q_ref, a * query_rows + at, query_frames) * (head_dim**-0.5)
            queries += [jnp.where(lane_head == h, q, 0.0) for h in range(HEADS)]
        keys = jnp.concatenate(keys, 0)
        queries = jnp.concatenate(queries, 0).astype(jnp.bfloat16)
        cross = lax.dot_general(keys, queries, NT, preferred_element_type=jnp.float32)
        scores = cross[:key_frames]
        for g in range(1, group):
            scores = jnp.where(lane_cell == g, cross[g * key_frames : (g + 1) * key_frames], scores)
        scores = scores * LOG2E
        mixed = jnp.zeros((key_frames, wide), jnp.float32)
        for back in range(REACH + 1):
            s = scores + bias_ref[back]
            e = jnp.exp2(s - jnp.max(s, axis=0, keepdims=True))
            z = jnp.sum(e, axis=0, keepdims=True)
            mixed = mixed + e * (coef_ref[back] / z)
        mixed = mixed.T.astype(jnp.bfloat16)
        for g in range(group):
            full = jnp.dot(
                mixed[g * span : (g + 1) * span], values[g], preferred_element_type=jnp.float32
            )
            out = full[:query_frames]
            for h in range(1, HEADS):
                out = jnp.where(lane_head == h, full[h * query_frames : (h + 1) * query_frames], out)
            rows = pl.ds(a * query_rows + first + g, query_frames, stride=half)
            for j in range(chunks):
                acc_ref[j, rows, :] = out[:, j * lanes : (j + 1) * lanes]

    for a in range(PACK):
        for first in range(0, half, group):
            group_step(a, first)
    quarter = query_rows // 4
    for i, out_ref in enumerate((own_ref, sib_ref, far_own_ref, far_sib_ref)):
        pieces = []
        for a in range(PACK):
            start = a * query_rows + i * quarter
            pieces.append([acc_ref[j, start : start + quarter] for j in range(chunks)])
        out_ref[...] = pack_lanes(*pieces).astype(out_ref.dtype)


def attend(parts, w_wide, ints, cells, planes):
    channels = w_wide.shape[1] // 3
    vmem = pl.BlockSpec(memory_space=pltpu.VMEM)
    _, rows, packed = parts[1].shape
    chunks = -(-channels // LANES)
    query_frames = 4 * rows * PACK // cells
    wide = GROUP * HEADS * query_frames
    keys, queries = 12 * rows * PACK, 4 * rows * PACK
    return pl.pallas_call(
        functools.partial(attend_kernel, cells, planes),
        out_shape=[jax.ShapeDtypeStruct((rows, packed), jnp.bfloat16)] * 4,
        in_specs=[vmem] * 12 + [pl.BlockSpec(memory_space=pl.ANY), vmem],
        out_specs=[vmem] * 4,
        scratch_shapes=[
            pltpu.SMEM(ints.shape, jnp.int32),
            pltpu.VMEM((keys, chunks * LANES), jnp.bfloat16),
            pltpu.VMEM((chunks, queries, LANES), jnp.float32),
            pltpu.VMEM((chunks, keys, LANES), jnp.float32),
            pltpu.VMEM((chunks, keys, LANES), jnp.float32),
            pltpu.VMEM((REACH + 1, 3 * query_frames, wide), jnp.float32),
            pltpu.VMEM((REACH + 1, 1, wide), jnp.float32),
            pltpu.VMEM((chunks, queries, LANES), jnp.float32),
            pltpu.SemaphoreType.DMA,
        ],
        compiler_params=pltpu.CompilerParams(vmem_limit_bytes=30 * 1024 * 1024),
        name="window_attention",
    )(*parts, ints, w_wide)


def group_mean(sums, spread, count):
    rows = sums.shape[0]
    high = sums.astype(jnp.bfloat16).astype(jnp.float32)
    mid = (sums - high).astype(jnp.bfloat16).astype(jnp.float32)
    parts = jnp.concatenate([high, mid, sums - high - mid], 0).astype(jnp.bfloat16)
    full = jnp.dot(parts, spread, preferred_element_type=jnp.float32)
    return (full[:rows] + full[rows : 2 * rows] + full[2 * rows :]) * (1.0 / count)


def group_act(rows, gain, spread, count):
    sums = sum(jnp.sum(row, axis=1) for row in rows)
    average = group_mean(sums, spread, count)
    cens = [row - average[:, None, :] for row in rows]
    variance = group_mean(sum(jnp.sum(cen * cen, axis=1) for cen in cens), spread, count)
    scale = lax.rsqrt(variance + EPS) * gain
    acts = []
    for cen in cens:
        v = cen * scale[:, None, :]
        acts.append(v / (1.0 + jnp.exp(-v)))
    return acts


def conv_rows(acts, w_ref, taps_ref):
    frames, cols, channels = acts[0].shape
    deep = w_ref.shape[2]
    count = len(acts)
    col = lax.broadcasted_iota(jnp.int32, (frames * cols, 1), 0) % cols
    for r, act in enumerate(acts):
        flat = act.reshape(frames * cols, channels)
        before = jnp.where(col == 0, 0.0, pltpu.roll(flat, 1, 0))
        after = jnp.where(col == cols - 1, 0.0, pltpu.roll(flat, frames * cols - 1, 0))
        for kw, part in enumerate((before, flat, after)):
            start = (3 * r + kw) * deep
            taps_ref[:, start : start + channels] = part.astype(jnp.bfloat16)
    outs = []
    for r in range(count):
        lo, hi = max(r - 1, 0), min(r + 1, count - 1)
        left = taps_ref[:, 3 * lo * deep : 3 * (hi + 1) * deep]
        right = w_ref[lo - r + 1 : hi - r + 2]
        right = right.reshape(-1, channels)
        out = jnp.dot(left, right, preferred_element_type=jnp.float32)
        outs.append(out.reshape(frames, cols, channels))
    return outs


def res_kernel(*refs):
    part_refs, (lat_ref, w_out_ref, gn_ref, one_ref, two_ref, out_ref) = refs[:4], refs[4:10]
    comb_ref, taps_ref = refs[10:]
    count, frames, cols, channels = lat_ref.shape
    deep = one_ref.shape[2]
    for i in range(3 * count):
        taps_ref[:, i * deep + channels : (i + 1) * deep] = jnp.zeros(
            (frames * cols, deep - channels), jnp.bfloat16
        )
    size = channels // NORM_GROUPS
    group_r = lax.broadcasted_iota(jnp.int32, (channels, 1), 0) // size
    group_c = lax.broadcasted_iota(jnp.int32, (1, channels), 1) // size
    spread = jnp.where(group_r == group_c, 1.0, 0.0).astype(jnp.bfloat16)
    members = count * cols * size

    core, chip, _ = place()
    half = comb_ref.shape[2] // PACK
    for i, (side, tall) in enumerate(
        ((core, chip), (1 - core, chip), (core, 1 - chip), (1 - core, 1 - chip))
    ):
        for a, piece in enumerate(unpack_lanes(part_refs[i][...].astype(jnp.float32))):
            piece = jnp.concatenate(piece, 1)[:, :channels].astype(jnp.bfloat16)
            comb_ref[:, side * 2 + tall, a * half : (a + 1) * half, :] = piece.reshape(
                frames, half, channels
            )
    combined = comb_ref[...].reshape(frames, count * cols, channels)
    hidden = []
    for r in range(count):
        comb = combined[:, r * cols : (r + 1) * cols, :].reshape(frames * cols, channels)
        proj = jnp.dot(comb, w_out_ref[:channels], preferred_element_type=jnp.float32)
        hid = lat_ref[r].astype(jnp.float32) + proj.reshape(frames, cols, channels)
        hidden.append(hid.astype(jnp.bfloat16).astype(jnp.float32))
    acts = group_act(hidden, gn_ref[0:1], spread, members)
    middle = [row + gn_ref[2:3][None] for row in conv_rows(acts, one_ref, taps_ref)]
    acts = group_act(middle, gn_ref[1:2], spread, members)
    for r, row in enumerate(conv_rows(acts, two_ref, taps_ref)):
        out_ref[:, r] = (hidden[r] + row).astype(out_ref.dtype)


def res_block(parts, extras):
    count, frames, cols, channels = extras[0].shape
    deep = -(-channels // LANES) * LANES
    vmem = pl.BlockSpec(memory_space=pltpu.VMEM)
    return pl.pallas_call(
        res_kernel,
        out_shape=jax.ShapeDtypeStruct((frames, count, cols, channels), jnp.bfloat16),
        in_specs=[vmem] * 9,
        out_specs=vmem,
        scratch_shapes=[
            pltpu.VMEM((frames, QUARTERS, count * cols // QUARTERS, channels), jnp.bfloat16),
            pltpu.VMEM((frames * cols, 3 * count * deep), jnp.bfloat16),
        ],
        compiler_params=pltpu.CompilerParams(vmem_limit_bytes=30 * 1024 * 1024),
        name="res_block",
    )(
        *parts,
        *extras,
    )


def body(
    latents, norm_gain, w_qkv, w_out, gn_gain, conv_one, conv_two, step_embed, offsets, numerators
):
    block_len, tile_rows, tile_cols, channels = latents.shape
    planes = lax.axis_size("frame") // QUARTERS
    cells = tile_rows * tile_cols // QUARTERS
    vmem = pl.BlockSpec(memory_space=pltpu.VMEM)
    rows, packed = block_len * cells // PACK, PACK * channels
    near, far = pl.pallas_call(
        pack_kernel,
        out_shape=[jax.ShapeDtypeStruct((2, rows, packed), jnp.bfloat16)] * 2,
        in_specs=[vmem] * 2,
        out_specs=[vmem] * 2,
        name="norm_pack",
    )(latents.reshape(block_len, QUARTERS, cells, channels), norm_gain)
    landed = [
        near,
        moved(far, lambda i: i ^ 2),
        moved(near, lambda i: i + QUARTERS),
        moved(far, lambda i: (i ^ 2) + QUARTERS),
        moved(near, lambda i: i - QUARTERS),
        moved(far, lambda i: (i ^ 2) - QUARTERS),
    ]
    more = (0, -channels % LANES)
    extras = [
        jnp.pad(w_qkv, (more, (0, 0))),
        jnp.concatenate([offsets, numerators]),
        latents.transpose(1, 0, 2, 3),
        jnp.pad(w_out, (more, (0, 0))),
        jnp.concatenate([gn_gain, step_embed[None]]),
        jnp.pad(conv_one, ((0, 0), (0, 0), more, (0, 0))),
        jnp.pad(conv_two, ((0, 0), (0, 0), more, (0, 0))),
    ]
    landed[1:4] = lax.optimization_barrier(landed[1:4])
    landed[0], extras = lax.optimization_barrier((near, extras))
    parts = []
    for piece in landed:
        parts += [piece, moved(piece, lambda i: i ^ 1)]
    parts[0] = parts[0][:1]
    w_wide, ints, *extras = extras
    own, sib, far_own, far_sib = attend(parts, w_wide, ints, cells, planes)
    pieces = [
        own,
        moved(sib, lambda i: i ^ 1),
        moved(far_own, lambda i: i ^ 2),
        moved(far_sib, lambda i: i ^ 3),
    ]
    return res_block(pieces, extras)


def solution(mesh):
    return jax.shard_map(
        body,
        mesh=mesh,
        in_specs=(
            P(("groups", "frame"), None, None, None),
            P(),
            P(),
            P(),
            P(),
            P(),
            P(),
            P(),
            P("groups"),
            P(),
        ),
        out_specs=P(("groups", "frame"), None, None, None),
        check_vma=False,
    )
```

```python
import functools

import jax
import jax.numpy as jnp
from jax import lax
from jax.experimental import pallas as pl
from jax.experimental.pallas import tpu as pltpu
from jax.sharding import PartitionSpec as P

HEADS = 5
NORM_GROUPS = 32
BLOCK = 4
WINDOW = 16
REACH = WINDOW // BLOCK
EPS = 1e-05
LANES = 128
GROUP = 2
LOG2E = 1.4426950408889634
NT = (((1,), (1,)), ((), ()))
QUARTERS = 4
PACK = 2


def place():
    me = lax.axis_index("frame")
    return me % 2, me // 2 % 2, me // QUARTERS


def moved(array, target):
    count = lax.axis_size("frame")
    return lax.ppermute(array, "frame", [(i, target(i) % count) for i in range(count)])


def pack_lanes(first, second):
    low = lax.broadcasted_iota(jnp.int32, first[-1].shape, first[-1].ndim - 1) < LANES // 2
    tail = jnp.where(low, first[-1], pltpu.roll(second[-1], LANES // 2, second[-1].ndim - 1))
    return jnp.concatenate(first[:-1] + second[:-1] + [tail], -1)


def unpack_lanes(rows):
    chunks = [rows[:, i : i + LANES] for i in range(0, rows.shape[1], LANES)]
    full = len(chunks) // 2
    low = lax.broadcasted_iota(jnp.int32, chunks[-1].shape, 1) < LANES // 2
    first = chunks[:full] + [jnp.where(low, chunks[-1], 0.0)]
    second = chunks[full:-1] + [jnp.where(low, pltpu.roll(chunks[-1], LANES // 2, 1), 0.0)]
    return first, second


def pack_kernel(lat_ref, gain_ref, near_ref, far_ref):
    core, chip, _ = place()
    frames, _, cells, channels = lat_ref.shape
    half = cells // PACK
    width = -(-channels // LANES) * LANES
    for out_ref, tall in ((near_ref, chip), (far_ref, 1 - chip)):
        for i, side in enumerate((core, 1 - core)):
            x = lat_ref[:, side * 2 + tall].astype(jnp.float32)
            cen = x - jnp.mean(x, axis=-1, keepdims=True)
            var = jnp.mean(cen * cen, axis=-1, keepdims=True)
            x = cen * lax.rsqrt(var + EPS) * gain_ref[...].reshape(1, 1, channels)
            x = jnp.concatenate([x, jnp.zeros((frames, cells, width - channels), x.dtype)], -1)
            halves = []
            for a in range(PACK):
                rows = x[:, a * half : (a + 1) * half].reshape(frames * half, width)
                halves.append([rows[:, j : j + LANES] for j in range(0, width, LANES)])
            out_ref[i] = pack_lanes(*halves).astype(out_ref.dtype)


def attend_kernel(cells, planes, *refs):
    sources, refs = refs[:12], refs[12:]
    ints_hbm, w_ref, own_ref, sib_ref, far_own_ref, far_sib_ref = refs[:6]
    (
        ints_ref, norm_ref, q_ref, k_ref, v_ref, bias_ref, coef_ref, acc_ref, sem,
    ) = refs[6:]
    core, chip, plane = place()
    channels = own_ref.shape[1] // PACK
    head_dim = channels // HEADS
    half = cells // PACK
    part_rows = sources[1].shape[1]
    part_frames = part_rows // half
    key_frames, query_frames = part_frames * 12, part_frames * 4
    key_rows, query_rows = key_frames * half, query_frames * half
    blocks = planes * QUARTERS
    frames = blocks * BLOCK
    group = GROUP
    wide = group * HEADS * query_frames
    chunks, lanes = k_ref.shape[0], k_ref.shape[2]
    copy = pltpu.make_async_copy(ints_hbm, ints_ref, sem)
    copy.start()

    for i in range(len(sources)):
        for a, x in enumerate(unpack_lanes(sources[i][i % 2].astype(jnp.float32))):
            start = a * key_rows + i * part_rows
            norm_ref[start : start + part_rows] = jnp.concatenate(x, 1).astype(jnp.bfloat16)
    pad = jnp.zeros((chunks * lanes, chunks * lanes - channels), jnp.bfloat16)
    for i, (out_ref, rows) in enumerate(((q_ref, query_rows), (k_ref, key_rows), (v_ref, key_rows))):
        w = jnp.concatenate([w_ref[:, i * channels : (i + 1) * channels], pad], 1)
        for a in range(PACK):
            here = norm_ref[a * key_rows : a * key_rows + rows]
            res = jnp.dot(here, w, preferred_element_type=jnp.float32)
            for j in range(chunks):
                out_ref[j, a * rows : (a + 1) * rows] = res[:, j * lanes : (j + 1) * lanes]

    copy.wait()
    ids = []
    for step in (0, planes - 1, 1):
        for tall in (chip, 1 - chip):
            base = lax.rem(plane + step, planes) * QUARTERS + 2 * tall
            ids += [base + core, base + 1 - core]
    lane = lax.broadcasted_iota(jnp.int32, (1, wide), 1)
    query = lane % query_frames
    block = jnp.zeros((1, wide), jnp.int32)
    for i in range(query_frames // BLOCK):
        block = jnp.where(query // BLOCK == i, ids[i], block)
    rest = query % BLOCK
    spot = lax.broadcasted_iota(jnp.int32, (key_frames, wide), 0)
    key = jnp.zeros((key_frames, wide), jnp.int32)
    for i, at in enumerate(ids):
        key = jnp.where(spot // BLOCK == i, at * BLOCK, key)
    key = key + spot % BLOCK
    weights = []
    for back in range(REACH + 1):
        owner = block - back
        owner = jnp.where(owner < 0, owner + blocks, owner)
        shift = jnp.zeros((1, wide), jnp.int32)
        for w in range(blocks):
            shift = jnp.where(owner == w, ints_ref[w], shift)
        at = BLOCK * back + rest - shift
        weight = jnp.zeros((1, wide), jnp.int32)
        for j in range(WINDOW):
            weight = jnp.where(at == j, ints_ref[blocks + j], weight)
        weights.append(weight.astype(jnp.float32))
        rel = key - (BLOCK * owner + shift)
        rel = jnp.where(rel < 0, rel + frames, rel)
        bias_ref[back] = jnp.where(rel < WINDOW, 0.0, -1e30)
    total = sum(weights)
    for back in range(REACH + 1):
        coef_ref[back] = weights[back] / total

    lane_head = lax.broadcasted_iota(jnp.int32, (1, chunks * lanes), 1) // head_dim
    lane_cell = lane // (HEADS * query_frames)
    span = HEADS * query_frames

    def rows_of(ref, start, size):
        rows = pl.ds(start, size, stride=half)
        return jnp.concatenate([ref[j, rows, :] for j in range(chunks)], 1)

    def group_step(a, first):
        keys, values, queries = [], [], []
        for g in range(group):
            at = first + g
            keys.append(rows_of(k_ref, a * key_rows + at, key_frames).astype(jnp.bfloat16))
            values.append(rows_of(v_ref, a * key_rows + at, key_frames).astype(jnp.bfloat16))
            q = rows_of(q_ref, a * query_rows + at, query_frames) * (head_dim**-0.5)
            queries += [jnp.where(lane_head == h, q, 0.0) for h in range(HEADS)]
        keys = jnp.concatenate(keys, 0)
        queries = jnp.concatenate(queries, 0).astype(jnp.bfloat16)
        cross = lax.dot_general(keys, queries, NT, preferred_element_type=jnp.float32)
        scores = cross[:key_frames]
        for g in range(1, group):
            scores = jnp.where(lane_cell == g, cross[g * key_frames : (g + 1) * key_frames], scores)
        scores = scores * LOG2E
        mixed = jnp.zeros((key_frames, wide), jnp.float32)
        for back in range(REACH + 1):
            s = scores + bias_ref[back]
            e = jnp.exp2(s - jnp.max(s, axis=0, keepdims=True))
            z = jnp.sum(e, axis=0, keepdims=True)
            mixed = mixed + e * (coef_ref[back] / z)
        mixed = mixed.T.astype(jnp.bfloat16)
        for g in range(group):
            full = jnp.dot(
                mixed[g * span : (g + 1) * span], values[g], preferred_element_type=jnp.float32
            )
            out = full[:query_frames]
            for h in range(1, HEADS):
                out = jnp.where(lane_head == h, full[h * query_frames : (h + 1) * query_frames], out)
            rows = pl.ds(a * query_rows + first + g, query_frames, stride=half)
            for j in range(chunks):
                acc_ref[j, rows, :] = out[:, j * lanes : (j + 1) * lanes]

    for a in range(PACK):
        for first in range(0, half, group):
            group_step(a, first)
    quarter = query_rows // 4
    for i, out_ref in enumerate((own_ref, sib_ref, far_own_ref, far_sib_ref)):
        pieces = []
        for a in range(PACK):
            start = a * query_rows + i * quarter
            pieces.append([acc_ref[j, start : start + quarter] for j in range(chunks)])
        out_ref[...] = pack_lanes(*pieces).astype(out_ref.dtype)


def attend(parts, w_wide, ints, cells, planes):
    channels = w_wide.shape[1] // 3
    vmem = pl.BlockSpec(memory_space=pltpu.VMEM)
    _, rows, packed = parts[1].shape
    chunks = -(-channels // LANES)
    query_frames = 4 * rows * PACK // cells
    wide = GROUP * HEADS * query_frames
    keys, queries = 12 * rows * PACK, 4 * rows * PACK
    return pl.pallas_call(
        functools.partial(attend_kernel, cells, planes),
        out_shape=[jax.ShapeDtypeStruct((rows, packed), jnp.bfloat16)] * 4,
        in_specs=[vmem] * 12 + [pl.BlockSpec(memory_space=pl.ANY), vmem],
        out_specs=[vmem] * 4,
        scratch_shapes=[
            pltpu.SMEM(ints.shape, jnp.int32),
            pltpu.VMEM((keys, chunks * LANES), jnp.bfloat16),
            pltpu.VMEM((chunks, queries, LANES), jnp.float32),
            pltpu.VMEM((chunks, keys, LANES), jnp.float32),
            pltpu.VMEM((chunks, keys, LANES), jnp.float32),
            pltpu.VMEM((REACH + 1, 3 * query_frames, wide), jnp.float32),
            pltpu.VMEM((REACH + 1, 1, wide), jnp.float32),
            pltpu.VMEM((chunks, queries, LANES), jnp.float32),
            pltpu.SemaphoreType.DMA,
        ],
        compiler_params=pltpu.CompilerParams(vmem_limit_bytes=30 * 1024 * 1024),
        name="window_attention",
    )(*parts, ints, w_wide)


def group_mean(sums, spread, count):
    rows = sums.shape[0]
    high = sums.astype(jnp.bfloat16).astype(jnp.float32)
    mid = (sums - high).astype(jnp.bfloat16).astype(jnp.float32)
    parts = jnp.concatenate([high, mid, sums - high - mid], 0).astype(jnp.bfloat16)
    full = jnp.dot(parts, spread, preferred_element_type=jnp.float32)
    return (full[:rows] + full[rows : 2 * rows] + full[2 * rows :]) * (1.0 / count)


def group_act(rows, gain, spread, count):
    sums = sum(jnp.sum(row, axis=1) for row in rows)
    average = group_mean(sums, spread, count)
    cens = [row - average[:, None, :] for row in rows]
    variance = group_mean(sum(jnp.sum(cen * cen, axis=1) for cen in cens), spread, count)
    scale = lax.rsqrt(variance + EPS) * gain
    acts = []
    for cen in cens:
        v = cen * scale[:, None, :]
        acts.append(v / (1.0 + jnp.exp(-v)))
    return acts


def conv_rows(acts, w_ref, taps_ref):
    frames, cols, channels = acts[0].shape
    deep = w_ref.shape[2]
    count = len(acts)
    col = lax.broadcasted_iota(jnp.int32, (frames * cols, 1), 0) % cols
    for r, act in enumerate(acts):
        flat = act.reshape(frames * cols, channels)
        before = jnp.where(col == 0, 0.0, pltpu.roll(flat, 1, 0))
        after = jnp.where(col == cols - 1, 0.0, pltpu.roll(flat, frames * cols - 1, 0))
        for kw, part in enumerate((before, flat, after)):
            start = (3 * r + kw) * deep
            taps_ref[:, start : start + channels] = part.astype(jnp.bfloat16)
    outs = []
    for r in range(count):
        lo, hi = max(r - 1, 0), min(r + 1, count - 1)
        left = taps_ref[:, 3 * lo * deep : 3 * (hi + 1) * deep]
        right = w_ref[lo - r + 1 : hi - r + 2]
        right = right.reshape(-1, channels)
        out = jnp.dot(left, right, preferred_element_type=jnp.float32)
        outs.append(out.reshape(frames, cols, channels))
    return outs


def res_kernel(*refs):
    part_refs, (lat_ref, w_out_ref, gn_ref, one_ref, two_ref, out_ref) = refs[:4], refs[4:10]
    comb_ref, taps_ref = refs[10:]
    count, frames, cols, channels = lat_ref.shape
    deep = one_ref.shape[2]
    for i in range(3 * count):
        taps_ref[:, i * deep + channels : (i + 1) * deep] = jnp.zeros(
            (frames * cols, deep - channels), jnp.bfloat16
        )
    size = channels // NORM_GROUPS
    group_r = lax.broadcasted_iota(jnp.int32, (channels, 1), 0) // size
    group_c = lax.broadcasted_iota(jnp.int32, (1, channels), 1) // size
    spread = jnp.where(group_r == group_c, 1.0, 0.0).astype(jnp.bfloat16)
    members = count * cols * size

    core, chip, _ = place()
    half = comb_ref.shape[2] // PACK
    for i, (side, tall) in enumerate(
        ((core, chip), (1 - core, chip), (core, 1 - chip), (1 - core, 1 - chip))
    ):
        for a, piece in enumerate(unpack_lanes(part_refs[i][...].astype(jnp.float32))):
            piece = jnp.concatenate(piece, 1)[:, :channels].astype(jnp.bfloat16)
            comb_ref[:, side * 2 + tall, a * half : (a + 1) * half, :] = piece.reshape(
                frames, half, channels
            )
    combined = comb_ref[...].reshape(frames, count * cols, channels)
    hidden = []
    for r in range(count):
        comb = combined[:, r * cols : (r + 1) * cols, :].reshape(frames * cols, channels)
        proj = jnp.dot(comb, w_out_ref[:channels], preferred_element_type=jnp.float32)
        hid = lat_ref[r].astype(jnp.float32) + proj.reshape(frames, cols, channels)
        hidden.append(hid.astype(jnp.bfloat16).astype(jnp.float32))
    acts = group_act(hidden, gn_ref[0:1], spread, members)
    middle = [row + gn_ref[2:3][None] for row in conv_rows(acts, one_ref, taps_ref)]
    acts = group_act(middle, gn_ref[1:2], spread, members)
    for r, row in enumerate(conv_rows(acts, two_ref, taps_ref)):
        out_ref[:, r] = (hidden[r] + row).astype(out_ref.dtype)


def res_block(parts, extras):
    count, frames, cols, channels = extras[0].shape
    deep = -(-channels // LANES) * LANES
    vmem = pl.BlockSpec(memory_space=pltpu.VMEM)
    return pl.pallas_call(
        res_kernel,
        out_shape=jax.ShapeDtypeStruct((frames, count, cols, channels), jnp.bfloat16),
        in_specs=[vmem] * 9,
        out_specs=vmem,
        scratch_shapes=[
            pltpu.VMEM((frames, QUARTERS, count * cols // QUARTERS, channels), jnp.bfloat16),
            pltpu.VMEM((frames * cols, 3 * count * deep), jnp.bfloat16),
        ],
        compiler_params=pltpu.CompilerParams(vmem_limit_bytes=30 * 1024 * 1024),
        name="res_block",
    )(
        *parts,
        *extras,
    )


def body(
    latents, norm_gain, w_qkv, w_out, gn_gain, conv_one, conv_two, step_embed, offsets, numerators
):
    block_len, tile_rows, tile_cols, channels = latents.shape
    planes = lax.axis_size("frame") // QUARTERS
    cells = tile_rows * tile_cols // QUARTERS
    vmem = pl.BlockSpec(memory_space=pltpu.VMEM)
    rows, packed = block_len * cells // PACK, PACK * channels
    near, far = pl.pallas_call(
        pack_kernel,
        out_shape=[jax.ShapeDtypeStruct((2, rows, packed), jnp.bfloat16)] * 2,
        in_specs=[vmem] * 2,
        out_specs=[vmem] * 2,
        name="norm_pack",
    )(latents.reshape(block_len, QUARTERS, cells, channels), norm_gain)
    landed = [
        near,
        moved(far, lambda i: i ^ 2),
        moved(near, lambda i: i + QUARTERS),
        moved(far, lambda i: (i ^ 2) + QUARTERS),
        moved(near, lambda i: i - QUARTERS),
        moved(far, lambda i: (i ^ 2) - QUARTERS),
    ]
    more = (0, -channels % LANES)
    extras = [
        jnp.pad(w_qkv, (more, (0, 0))),
        jnp.concatenate([offsets, numerators]),
        latents.transpose(1, 0, 2, 3),
        jnp.pad(w_out, (more, (0, 0))),
        jnp.concatenate([gn_gain, step_embed[None]]),
        jnp.pad(conv_one, ((0, 0), (0, 0), more, (0, 0))),
        jnp.pad(conv_two, ((0, 0), (0, 0), more, (0, 0))),
    ]
    landed[2], extras = lax.optimization_barrier((landed[2], extras))
    parts = []
    for piece in landed:
        parts += [piece, moved(piece, lambda i: i ^ 1)]
    parts[0] = parts[0][:1]
    w_wide, ints, *extras = extras
    own, sib, far_own, far_sib = attend(parts, w_wide, ints, cells, planes)
    pieces = [
        own,
        moved(sib, lambda i: i ^ 1),
        moved(far_own, lambda i: i ^ 2),
        moved(far_sib, lambda i: i ^ 3),
    ]
    return res_block(pieces, extras)


def solution(mesh):
    return jax.shard_map(
        body,
        mesh=mesh,
        in_specs=(
            P(("groups", "frame"), None, None, None),
            P(),
            P(),
            P(),
            P(),
            P(),
            P(),
            P(),
            P("groups"),
            P(),
        ),
        out_specs=P(("groups", "frame"), None, None, None),
        check_vma=False,
    )
```

```python
import functools

import jax
import jax.numpy as jnp
from jax import lax
from jax.experimental import pallas as pl
from jax.experimental.pallas import tpu as pltpu
from jax.sharding import PartitionSpec as P

HEADS = 5
NORM_GROUPS = 32
BLOCK = 4
WINDOW = 16
REACH = WINDOW // BLOCK
EPS = 1e-05
LANES = 128
GROUP = 2
LOG2E = 1.4426950408889634
NT = (((1,), (1,)), ((), ()))
QUARTERS = 4
PACK = 2


def place():
    me = lax.axis_index("frame")
    return me % 2, me // 2 % 2, me // QUARTERS


def moved(array, target):
    count = lax.axis_size("frame")
    return lax.ppermute(array, "frame", [(i, target(i) % count) for i in range(count)])


def pack_lanes(first, second):
    low = lax.broadcasted_iota(jnp.int32, first[-1].shape, first[-1].ndim - 1) < LANES // 2
    tail = jnp.where(low, first[-1], pltpu.roll(second[-1], LANES // 2, second[-1].ndim - 1))
    return jnp.concatenate(first[:-1] + second[:-1] + [tail], -1)


def unpack_lanes(rows):
    chunks = [rows[:, i : i + LANES] for i in range(0, rows.shape[1], LANES)]
    full = len(chunks) // 2
    low = lax.broadcasted_iota(jnp.int32, chunks[-1].shape, 1) < LANES // 2
    first = chunks[:full] + [jnp.where(low, chunks[-1], 0.0)]
    second = chunks[full:-1] + [jnp.where(low, pltpu.roll(chunks[-1], LANES // 2, 1), 0.0)]
    return first, second


def pack_kernel(lat_ref, gain_ref, near_ref, far_ref):
    core, chip, _ = place()
    frames, _, cells, channels = lat_ref.shape
    half = cells // PACK
    width = -(-channels // LANES) * LANES
    for out_ref, tall in ((near_ref, chip), (far_ref, 1 - chip)):
        for i, side in enumerate((core, 1 - core)):
            x = lat_ref[:, side * 2 + tall].astype(jnp.float32)
            cen = x - jnp.mean(x, axis=-1, keepdims=True)
            var = jnp.mean(cen * cen, axis=-1, keepdims=True)
            x = cen * lax.rsqrt(var + EPS) * gain_ref[...].reshape(1, 1, channels)
            x = jnp.concatenate([x, jnp.zeros((frames, cells, width - channels), x.dtype)], -1)
            halves = []
            for a in range(PACK):
                rows = x[:, a * half : (a + 1) * half].reshape(frames * half, width)
                halves.append([rows[:, j : j + LANES] for j in range(0, width, LANES)])
            out_ref[i] = pack_lanes(*halves).astype(out_ref.dtype)


def attend_kernel(cells, planes, *refs):
    sources, refs = refs[:12], refs[12:]
    ints_hbm, w_ref, own_ref, sib_ref, far_own_ref, far_sib_ref = refs[:6]
    (
        ints_ref, norm_ref, q_ref, k_ref, v_ref, bias_ref, coef_ref, acc_ref, sem,
    ) = refs[6:]
    core, chip, plane = place()
    channels = own_ref.shape[1] // PACK
    head_dim = channels // HEADS
    half = cells // PACK
    part_rows = sources[1].shape[1]
    part_frames = part_rows // half
    key_frames, query_frames = part_frames * 12, part_frames * 4
    key_rows, query_rows = key_frames * half, query_frames * half
    blocks = planes * QUARTERS
    frames = blocks * BLOCK
    group = GROUP
    wide = group * HEADS * query_frames
    chunks, lanes = k_ref.shape[0], k_ref.shape[2]
    copy = pltpu.make_async_copy(ints_hbm, ints_ref, sem)
    copy.start()

    for i in range(len(sources)):
        for a, x in enumerate(unpack_lanes(sources[i][i % 2].astype(jnp.float32))):
            start = a * key_rows + i * part_rows
            norm_ref[start : start + part_rows] = jnp.concatenate(x, 1).astype(jnp.bfloat16)
    pad = jnp.zeros((chunks * lanes, chunks * lanes - channels), jnp.bfloat16)
    for i, (out_ref, rows) in enumerate(((q_ref, query_rows), (k_ref, key_rows), (v_ref, key_rows))):
        w = jnp.concatenate([w_ref[:, i * channels : (i + 1) * channels], pad], 1)
        for a in range(PACK):
            here = norm_ref[a * key_rows : a * key_rows + rows]
            res = jnp.dot(here, w, preferred_element_type=jnp.float32)
            for j in range(chunks):
                out_ref[j, a * rows : (a + 1) * rows] = res[:, j * lanes : (j + 1) * lanes]

    copy.wait()
    ids = []
    for step in (0, planes - 1, 1):
        for tall in (chip, 1 - chip):
            base = lax.rem(plane + step, planes) * QUARTERS + 2 * tall
            ids += [base + core, base + 1 - core]
    lane = lax.broadcasted_iota(jnp.int32, (1, wide), 1)
    query = lane % query_frames
    block = jnp.zeros((1, wide), jnp.int32)
    for i in range(query_frames // BLOCK):
        block = jnp.where(query // BLOCK == i, ids[i], block)
    rest = query % BLOCK
    spot = lax.broadcasted_iota(jnp.int32, (key_frames, wide), 0)
    key = jnp.zeros((key_frames, wide), jnp.int32)
    for i, at in enumerate(ids):
        key = jnp.where(spot // BLOCK == i, at * BLOCK, key)
    key = key + spot % BLOCK
    weights = []
    for back in range(REACH + 1):
        owner = block - back
        owner = jnp.where(owner < 0, owner + blocks, owner)
        shift = jnp.zeros((1, wide), jnp.int32)
        for w in range(blocks):
            shift = jnp.where(owner == w, ints_ref[w], shift)
        at = BLOCK * back + rest - shift
        weight = jnp.zeros((1, wide), jnp.int32)
        for j in range(WINDOW):
            weight = jnp.where(at == j, ints_ref[blocks + j], weight)
        weights.append(weight.astype(jnp.float32))
        rel = key - (BLOCK * owner + shift)
        rel = jnp.where(rel < 0, rel + frames, rel)
        bias_ref[back] = jnp.where(rel < WINDOW, 0.0, -1e30)
    total = sum(weights)
    for back in range(REACH + 1):
        coef_ref[back] = weights[back] / total

    lane_head = lax.broadcasted_iota(jnp.int32, (1, chunks * lanes), 1) // head_dim
    lane_cell = lane // (HEADS * query_frames)
    span = HEADS * query_frames

    def rows_of(ref, start, size):
        rows = pl.ds(start, size, stride=half)
        return jnp.concatenate([ref[j, rows, :] for j in range(chunks)], 1)

    def group_step(a, first):
        keys, values, queries = [], [], []
        for g in range(group):
            at = first + g
            keys.append(rows_of(k_ref, a * key_rows + at, key_frames).astype(jnp.bfloat16))
            values.append(rows_of(v_ref, a * key_rows + at, key_frames).astype(jnp.bfloat16))
            q = rows_of(q_ref, a * query_rows + at, query_frames) * (head_dim**-0.5)
            queries += [jnp.where(lane_head == h, q, 0.0) for h in range(HEADS)]
        keys = jnp.concatenate(keys, 0)
        queries = jnp.concatenate(queries, 0).astype(jnp.bfloat16)
        cross = lax.dot_general(keys, queries, NT, preferred_element_type=jnp.float32)
        scores = cross[:key_frames]
        for g in range(1, group):
            scores = jnp.where(lane_cell == g, cross[g * key_frames : (g + 1) * key_frames], scores)
        scores = scores * LOG2E
        mixed = jnp.zeros((key_frames, wide), jnp.float32)
        for back in range(REACH + 1):
            third = key_frames // 3
            spans = {0: ((0, third), (2 * third, key_frames)), REACH: ((0, 2 * third),)}
            spans = spans.get(back, ((0, key_frames),))
            s = jnp.concatenate([scores[lo:hi] + bias_ref[back, lo:hi] for lo, hi in spans], 0)
            e = jnp.exp2(s - jnp.max(s, axis=0, keepdims=True))
            z = jnp.sum(e, axis=0, keepdims=True)
            e = e * (coef_ref[back] / z)
            if back == 0:
                none = jnp.zeros((third, wide), jnp.float32)
                e = jnp.concatenate([e[:third], none, e[third:]], 0)
            elif back == REACH:
                e = jnp.concatenate([e, jnp.zeros((third, wide), jnp.float32)], 0)
            mixed = mixed + e
        mixed = mixed.T.astype(jnp.bfloat16)
        for g in range(group):
            full = jnp.dot(
                mixed[g * span : (g + 1) * span], values[g], preferred_element_type=jnp.float32
            )
            out = full[:query_frames]
            for h in range(1, HEADS):
                out = jnp.where(lane_head == h, full[h * query_frames : (h + 1) * query_frames], out)
            rows = pl.ds(a * query_rows + first + g, query_frames, stride=half)
            for j in range(chunks):
                acc_ref[j, rows, :] = out[:, j * lanes : (j + 1) * lanes]

    for a in range(PACK):
        for first in range(0, half, group):
            group_step(a, first)
    quarter = query_rows // 4
    for i, out_ref in enumerate((own_ref, sib_ref, far_own_ref, far_sib_ref)):
        pieces = []
        for a in range(PACK):
            start = a * query_rows + i * quarter
            pieces.append([acc_ref[j, start : start + quarter] for j in range(chunks)])
        out_ref[...] = pack_lanes(*pieces).astype(out_ref.dtype)


def attend(parts, w_wide, ints, cells, planes):
    channels = w_wide.shape[1] // 3
    vmem = pl.BlockSpec(memory_space=pltpu.VMEM)
    _, rows, packed = parts[1].shape
    chunks = -(-channels // LANES)
    query_frames = 4 * rows * PACK // cells
    wide = GROUP * HEADS * query_frames
    keys, queries = 12 * rows * PACK, 4 * rows * PACK
    return pl.pallas_call(
        functools.partial(attend_kernel, cells, planes),
        out_shape=[jax.ShapeDtypeStruct((rows, packed), jnp.bfloat16)] * 4,
        in_specs=[vmem] * 12 + [pl.BlockSpec(memory_space=pl.ANY), vmem],
        out_specs=[vmem] * 4,
        scratch_shapes=[
            pltpu.SMEM(ints.shape, jnp.int32),
            pltpu.VMEM((keys, chunks * LANES), jnp.bfloat16),
            pltpu.VMEM((chunks, queries, LANES), jnp.float32),
            pltpu.VMEM((chunks, keys, LANES), jnp.float32),
            pltpu.VMEM((chunks, keys, LANES), jnp.float32),
            pltpu.VMEM((REACH + 1, 3 * query_frames, wide), jnp.float32),
            pltpu.VMEM((REACH + 1, 1, wide), jnp.float32),
            pltpu.VMEM((chunks, queries, LANES), jnp.float32),
            pltpu.SemaphoreType.DMA,
        ],
        compiler_params=pltpu.CompilerParams(vmem_limit_bytes=30 * 1024 * 1024),
        name="window_attention",
    )(*parts, ints, w_wide)


def group_mean(sums, spread, count):
    rows = sums.shape[0]
    high = sums.astype(jnp.bfloat16).astype(jnp.float32)
    mid = (sums - high).astype(jnp.bfloat16).astype(jnp.float32)
    parts = jnp.concatenate([high, mid, sums - high - mid], 0).astype(jnp.bfloat16)
    full = jnp.dot(parts, spread, preferred_element_type=jnp.float32)
    return (full[:rows] + full[rows : 2 * rows] + full[2 * rows :]) * (1.0 / count)


def group_act(rows, gain, spread, count):
    sums = sum(jnp.sum(row, axis=1) for row in rows)
    average = group_mean(sums, spread, count)
    cens = [row - average[:, None, :] for row in rows]
    variance = group_mean(sum(jnp.sum(cen * cen, axis=1) for cen in cens), spread, count)
    scale = lax.rsqrt(variance + EPS) * gain
    acts = []
    for cen in cens:
        v = cen * scale[:, None, :]
        acts.append(v / (1.0 + jnp.exp(-v)))
    return acts


def conv_rows(acts, w_ref, taps_ref):
    frames, cols, channels = acts[0].shape
    deep = w_ref.shape[2]
    count = len(acts)
    col = lax.broadcasted_iota(jnp.int32, (frames * cols, 1), 0) % cols
    for r, act in enumerate(acts):
        flat = act.reshape(frames * cols, channels)
        before = jnp.where(col == 0, 0.0, pltpu.roll(flat, 1, 0))
        after = jnp.where(col == cols - 1, 0.0, pltpu.roll(flat, frames * cols - 1, 0))
        for kw, part in enumerate((before, flat, after)):
            start = (3 * r + kw) * deep
            taps_ref[:, start : start + channels] = part.astype(jnp.bfloat16)
    outs = []
    for r in range(count):
        lo, hi = max(r - 1, 0), min(r + 1, count - 1)
        left = taps_ref[:, 3 * lo * deep : 3 * (hi + 1) * deep]
        right = w_ref[lo - r + 1 : hi - r + 2]
        right = right.reshape(-1, channels)
        out = jnp.dot(left, right, preferred_element_type=jnp.float32)
        outs.append(out.reshape(frames, cols, channels))
    return outs


def res_kernel(*refs):
    part_refs, (lat_ref, w_out_ref, gn_ref, one_ref, two_ref, out_ref) = refs[:4], refs[4:10]
    comb_ref, taps_ref = refs[10:]
    count, frames, cols, channels = lat_ref.shape
    deep = one_ref.shape[2]
    for i in range(3 * count):
        taps_ref[:, i * deep + channels : (i + 1) * deep] = jnp.zeros(
            (frames * cols, deep - channels), jnp.bfloat16
        )
    size = channels // NORM_GROUPS
    group_r = lax.broadcasted_iota(jnp.int32, (channels, 1), 0) // size
    group_c = lax.broadcasted_iota(jnp.int32, (1, channels), 1) // size
    spread = jnp.where(group_r == group_c, 1.0, 0.0).astype(jnp.bfloat16)
    members = count * cols * size

    core, chip, _ = place()
    half = comb_ref.shape[2] // PACK
    for i, (side, tall) in enumerate(
        ((core, chip), (1 - core, chip), (core, 1 - chip), (1 - core, 1 - chip))
    ):
        for a, piece in enumerate(unpack_lanes(part_refs[i][...].astype(jnp.float32))):
            piece = jnp.concatenate(piece, 1)[:, :channels].astype(jnp.bfloat16)
            comb_ref[:, side * 2 + tall, a * half : (a + 1) * half, :] = piece.reshape(
                frames, half, channels
            )
    combined = comb_ref[...].reshape(frames, count * cols, channels)
    hidden = []
    for r in range(count):
        comb = combined[:, r * cols : (r + 1) * cols, :].reshape(frames * cols, channels)
        proj = jnp.dot(comb, w_out_ref[:channels], preferred_element_type=jnp.float32)
        hid = lat_ref[r].astype(jnp.float32) + proj.reshape(frames, cols, channels)
        hidden.append(hid.astype(jnp.bfloat16).astype(jnp.float32))
    acts = group_act(hidden, gn_ref[0:1], spread, members)
    middle = [row + gn_ref[2:3][None] for row in conv_rows(acts, one_ref, taps_ref)]
    acts = group_act(middle, gn_ref[1:2], spread, members)
    for r, row in enumerate(conv_rows(acts, two_ref, taps_ref)):
        out_ref[:, r] = (hidden[r] + row).astype(out_ref.dtype)


def res_block(parts, extras):
    count, frames, cols, channels = extras[0].shape
    deep = -(-channels // LANES) * LANES
    vmem = pl.BlockSpec(memory_space=pltpu.VMEM)
    return pl.pallas_call(
        res_kernel,
        out_shape=jax.ShapeDtypeStruct((frames, count, cols, channels), jnp.bfloat16),
        in_specs=[vmem] * 9,
        out_specs=vmem,
        scratch_shapes=[
            pltpu.VMEM((frames, QUARTERS, count * cols // QUARTERS, channels), jnp.bfloat16),
            pltpu.VMEM((frames * cols, 3 * count * deep), jnp.bfloat16),
        ],
        compiler_params=pltpu.CompilerParams(vmem_limit_bytes=30 * 1024 * 1024),
        name="res_block",
    )(
        *parts,
        *extras,
    )


def body(
    latents, norm_gain, w_qkv, w_out, gn_gain, conv_one, conv_two, step_embed, offsets, numerators
):
    block_len, tile_rows, tile_cols, channels = latents.shape
    planes = lax.axis_size("frame") // QUARTERS
    cells = tile_rows * tile_cols // QUARTERS
    vmem = pl.BlockSpec(memory_space=pltpu.VMEM)
    rows, packed = block_len * cells // PACK, PACK * channels
    near, far = pl.pallas_call(
        pack_kernel,
        out_shape=[jax.ShapeDtypeStruct((2, rows, packed), jnp.bfloat16)] * 2,
        in_specs=[vmem] * 2,
        out_specs=[vmem] * 2,
        name="norm_pack",
    )(latents.reshape(block_len, QUARTERS, cells, channels), norm_gain)
    landed = [
        near,
        moved(far, lambda i: i ^ 2),
        moved(near, lambda i: i + QUARTERS),
        moved(far, lambda i: (i ^ 2) + QUARTERS),
        moved(near, lambda i: i - QUARTERS),
        moved(far, lambda i: (i ^ 2) - QUARTERS),
    ]
    more = (0, -channels % LANES)
    extras = [
        jnp.pad(w_qkv, (more, (0, 0))),
        jnp.concatenate([offsets, numerators]),
        latents.transpose(1, 0, 2, 3),
        jnp.pad(w_out, (more, (0, 0))),
        jnp.concatenate([gn_gain, step_embed[None]]),
        jnp.pad(conv_one, ((0, 0), (0, 0), more, (0, 0))),
        jnp.pad(conv_two, ((0, 0), (0, 0), more, (0, 0))),
    ]
    landed[2], extras = lax.optimization_barrier((landed[2], extras))
    parts = []
    for piece in landed:
        parts += [piece, moved(piece, lambda i: i ^ 1)]
    parts[0] = parts[0][:1]
    w_wide, ints, *extras = extras
    own, sib, far_own, far_sib = attend(parts, w_wide, ints, cells, planes)
    pieces = [
        own,
        moved(sib, lambda i: i ^ 1),
        moved(far_own, lambda i: i ^ 2),
        moved(far_sib, lambda i: i ^ 3),
    ]
    return res_block(pieces, extras)


def solution(mesh):
    return jax.shard_map(
        body,
        mesh=mesh,
        in_specs=(
            P(("groups", "frame"), None, None, None),
            P(),
            P(),
            P(),
            P(),
            P(),
            P(),
            P(),
            P("groups"),
            P(),
        ),
        out_specs=P(("groups", "frame"), None, None, None),
        check_vma=False,
    )
```

```python
import functools

import jax
import jax.numpy as jnp
from jax import lax
from jax.experimental import pallas as pl
from jax.experimental.pallas import tpu as pltpu
from jax.sharding import PartitionSpec as P

HEADS = 5
NORM_GROUPS = 32
BLOCK = 4
WINDOW = 16
REACH = WINDOW // BLOCK
EPS = 1e-05
LANES = 128
GROUP = 2
LOG2E = 1.4426950408889634
NT = (((1,), (1,)), ((), ()))
QUARTERS = 4
PACK = 2


def place():
    me = lax.axis_index("frame")
    return me % 2, me // 2 % 2, me // QUARTERS


def moved(array, target):
    count = lax.axis_size("frame")
    return lax.ppermute(array, "frame", [(i, target(i) % count) for i in range(count)])


def pack_lanes(first, second):
    low = lax.broadcasted_iota(jnp.int32, first[-1].shape, first[-1].ndim - 1) < LANES // 2
    tail = jnp.where(low, first[-1], pltpu.roll(second[-1], LANES // 2, second[-1].ndim - 1))
    return jnp.concatenate(first[:-1] + second[:-1] + [tail], -1)


def unpack_lanes(rows):
    chunks = [rows[:, i : i + LANES] for i in range(0, rows.shape[1], LANES)]
    full = len(chunks) // 2
    low = lax.broadcasted_iota(jnp.int32, chunks[-1].shape, 1) < LANES // 2
    first = chunks[:full] + [jnp.where(low, chunks[-1], 0.0)]
    second = chunks[full:-1] + [jnp.where(low, pltpu.roll(chunks[-1], LANES // 2, 1), 0.0)]
    return first, second


def pack_kernel(lat_ref, gain_ref, near_ref, far_ref):
    core, chip, _ = place()
    frames, _, cells, channels = lat_ref.shape
    half = cells // PACK
    width = -(-channels // LANES) * LANES
    for out_ref, tall in ((near_ref, chip), (far_ref, 1 - chip)):
        for i, side in enumerate((core, 1 - core)):
            x = lat_ref[:, side * 2 + tall].astype(jnp.float32)
            cen = x - jnp.mean(x, axis=-1, keepdims=True)
            var = jnp.mean(cen * cen, axis=-1, keepdims=True)
            x = cen * lax.rsqrt(var + EPS) * gain_ref[...].reshape(1, 1, channels)
            x = jnp.concatenate([x, jnp.zeros((frames, cells, width - channels), x.dtype)], -1)
            halves = []
            for a in range(PACK):
                rows = x[:, a * half : (a + 1) * half].reshape(frames * half, width)
                halves.append([rows[:, j : j + LANES] for j in range(0, width, LANES)])
            out_ref[i] = pack_lanes(*halves).astype(out_ref.dtype)


def attend_kernel(cells, planes, *refs):
    sources, refs = refs[:12], refs[12:]
    ints_hbm, w_ref, own_ref, sib_ref, far_own_ref, far_sib_ref = refs[:6]
    (
        ints_ref, norm_ref, q_ref, k_ref, v_ref, bias_ref, coef_ref, acc_ref, sem,
    ) = refs[6:]
    core, chip, plane = place()
    channels = own_ref.shape[1] // PACK
    head_dim = channels // HEADS
    half = cells // PACK
    part_rows = sources[1].shape[1]
    part_frames = part_rows // half
    key_frames, query_frames = part_frames * 12, part_frames * 4
    key_rows, query_rows = key_frames * half, query_frames * half
    blocks = planes * QUARTERS
    frames = blocks * BLOCK
    group = GROUP
    wide = group * HEADS * query_frames
    chunks, lanes = k_ref.shape[0], k_ref.shape[2]
    copy = pltpu.make_async_copy(ints_hbm, ints_ref, sem)
    copy.start()

    for i in range(len(sources)):
        for a, x in enumerate(unpack_lanes(sources[i][i % 2].astype(jnp.float32))):
            start = a * key_rows + i * part_rows
            norm_ref[start : start + part_rows] = jnp.concatenate(x, 1).astype(jnp.bfloat16)
    pad = jnp.zeros((chunks * lanes, chunks * lanes - channels), jnp.bfloat16)
    for i, (out_ref, rows) in enumerate(((q_ref, query_rows), (k_ref, key_rows), (v_ref, key_rows))):
        w = jnp.concatenate([w_ref[:, i * channels : (i + 1) * channels], pad], 1)
        for a in range(PACK):
            here = norm_ref[a * key_rows : a * key_rows + rows]
            res = jnp.dot(here, w, preferred_element_type=jnp.float32)
            for j in range(chunks):
                out_ref[j, a * rows : (a + 1) * rows] = res[:, j * lanes : (j + 1) * lanes]

    copy.wait()
    ids = []
    for step in (0, planes - 1, 1):
        for tall in (chip, 1 - chip):
            base = lax.rem(plane + step, planes) * QUARTERS + 2 * tall
            ids += [base + core, base + 1 - core]
    lane = lax.broadcasted_iota(jnp.int32, (1, wide), 1)
    query = lane % query_frames
    block = jnp.zeros((1, wide), jnp.int32)
    for i in range(query_frames // BLOCK):
        block = jnp.where(query // BLOCK == i, ids[i], block)
    rest = query % BLOCK
    spot = lax.broadcasted_iota(jnp.int32, (key_frames, wide), 0)
    key = jnp.zeros((key_frames, wide), jnp.int32)
    for i, at in enumerate(ids):
        key = jnp.where(spot // BLOCK == i, at * BLOCK, key)
    key = key + spot % BLOCK
    weights = []
    for back in range(REACH + 1):
        owner = block - back
        owner = jnp.where(owner < 0, owner + blocks, owner)
        shift = jnp.zeros((1, wide), jnp.int32)
        for w in range(blocks):
            shift = jnp.where(owner == w, ints_ref[w], shift)
        at = BLOCK * back + rest - shift
        weight = jnp.zeros((1, wide), jnp.int32)
        for j in range(WINDOW):
            weight = jnp.where(at == j, ints_ref[blocks + j], weight)
        weights.append(weight.astype(jnp.float32))
        rel = key - (BLOCK * owner + shift)
        rel = jnp.where(rel < 0, rel + frames, rel)
        bias_ref[back] = jnp.where(rel < WINDOW, 0.0, -1e30)
    total = sum(weights)
    for back in range(REACH + 1):
        coef_ref[back] = weights[back] / total

    lane_head = lax.broadcasted_iota(jnp.int32, (1, chunks * lanes), 1) // head_dim
    lane_cell = lane // (HEADS * query_frames)
    span = HEADS * query_frames

    def rows_of(ref, start, size):
        rows = pl.ds(start, size, stride=half)
        return jnp.concatenate([ref[j, rows, :] for j in range(chunks)], 1)

    def group_step(a, first):
        keys, values, queries = [], [], []
        for g in range(group):
            at = first + g
            keys.append(rows_of(k_ref, a * key_rows + at, key_frames).astype(jnp.bfloat16))
            values.append(rows_of(v_ref, a * key_rows + at, key_frames).astype(jnp.bfloat16))
            q = rows_of(q_ref, a * query_rows + at, query_frames) * (head_dim**-0.5)
            queries += [jnp.where(lane_head == h, q, 0.0) for h in range(HEADS)]
        keys = jnp.concatenate(keys, 0)
        queries = jnp.concatenate(queries, 0).astype(jnp.bfloat16)
        cross = lax.dot_general(keys, queries, NT, preferred_element_type=jnp.float32)
        scores = cross[:key_frames]
        for g in range(1, group):
            scores = jnp.where(lane_cell == g, cross[g * key_frames : (g + 1) * key_frames], scores)
        scores = scores * LOG2E
        mixed = jnp.zeros((key_frames, wide), jnp.float32)
        for back in range(REACH + 1):
            third = key_frames // 3
            spans = {0: ((0, third), (2 * third, key_frames)), REACH: ((0, 2 * third),)}
            spans = spans.get(back, ((0, key_frames),))
            s = jnp.concatenate([scores[lo:hi] + bias_ref[back, lo:hi] for lo, hi in spans], 0)
            e = jnp.exp2(s - jnp.max(s, axis=0, keepdims=True))
            z = jnp.sum(e, axis=0, keepdims=True)
            e = e * (coef_ref[back] / z)
            if back == 0:
                none = jnp.zeros((third, wide), jnp.float32)
                e = jnp.concatenate([e[:third], none, e[third:]], 0)
            elif back == REACH:
                e = jnp.concatenate([e, jnp.zeros((third, wide), jnp.float32)], 0)
            mixed = mixed + e
        mixed = mixed.T.astype(jnp.bfloat16)
        for g in range(group):
            full = jnp.dot(
                mixed[g * span : (g + 1) * span], values[g], preferred_element_type=jnp.float32
            )
            out = full[:query_frames]
            for h in range(1, HEADS):
                out = jnp.where(lane_head == h, full[h * query_frames : (h + 1) * query_frames], out)
            rows = pl.ds(a * query_rows + first + g, query_frames, stride=half)
            for j in range(chunks):
                acc_ref[j, rows, :] = out[:, j * lanes : (j + 1) * lanes]

    for a in range(PACK):
        for first in range(0, half, group):
            group_step(a, first)
    quarter = query_rows // 4
    for i, out_ref in enumerate((own_ref, sib_ref, far_own_ref, far_sib_ref)):
        pieces = []
        for a in range(PACK):
            start = a * query_rows + i * quarter
            pieces.append([acc_ref[j, start : start + quarter] for j in range(chunks)])
        out_ref[...] = pack_lanes(*pieces).astype(out_ref.dtype)


def attend(parts, w_wide, ints, cells, planes):
    channels = w_wide.shape[1] // 3
    vmem = pl.BlockSpec(memory_space=pltpu.VMEM)
    _, rows, packed = parts[1].shape
    chunks = -(-channels // LANES)
    query_frames = 4 * rows * PACK // cells
    wide = GROUP * HEADS * query_frames
    keys, queries = 12 * rows * PACK, 4 * rows * PACK
    return pl.pallas_call(
        functools.partial(attend_kernel, cells, planes),
        out_shape=[jax.ShapeDtypeStruct((rows, packed), jnp.bfloat16)] * 4,
        in_specs=[vmem] * 12 + [pl.BlockSpec(memory_space=pl.ANY), vmem],
        out_specs=[vmem] * 4,
        scratch_shapes=[
            pltpu.SMEM(ints.shape, jnp.int32),
            pltpu.VMEM((keys, chunks * LANES), jnp.bfloat16),
            pltpu.VMEM((chunks, queries, LANES), jnp.float32),
            pltpu.VMEM((chunks, keys, LANES), jnp.float32),
            pltpu.VMEM((chunks, keys, LANES), jnp.float32),
            pltpu.VMEM((REACH + 1, 3 * query_frames, wide), jnp.float32),
            pltpu.VMEM((REACH + 1, 1, wide), jnp.float32),
            pltpu.VMEM((chunks, queries, LANES), jnp.float32),
            pltpu.SemaphoreType.DMA,
        ],
        compiler_params=pltpu.CompilerParams(vmem_limit_bytes=30 * 1024 * 1024),
        name="window_attention",
    )(*parts, ints, w_wide)


def group_mean(sums, spread, count):
    rows = sums.shape[0]
    high = sums.astype(jnp.bfloat16).astype(jnp.float32)
    mid = (sums - high).astype(jnp.bfloat16).astype(jnp.float32)
    parts = jnp.concatenate([high, mid, sums - high - mid], 0).astype(jnp.bfloat16)
    full = jnp.dot(parts, spread, preferred_element_type=jnp.float32)
    return (full[:rows] + full[rows : 2 * rows] + full[2 * rows :]) * (1.0 / count)


def group_act(rows, gain, spread, count):
    sums = sum(jnp.sum(row, axis=1) for row in rows)
    average = group_mean(sums, spread, count)
    cens = [row - average[:, None, :] for row in rows]
    variance = group_mean(sum(jnp.sum(cen * cen, axis=1) for cen in cens), spread, count)
    scale = lax.rsqrt(variance + EPS) * gain
    acts = []
    for cen in cens:
        v = cen * scale[:, None, :]
        acts.append(v / (1.0 + jnp.exp(-v)))
    return acts


def conv_rows(acts, w_ref, taps_ref):
    frames, cols, channels = acts[0].shape
    deep = w_ref.shape[2]
    count = len(acts)
    col = lax.broadcasted_iota(jnp.int32, (frames * cols, 1), 0) % cols
    for r, act in enumerate(acts):
        flat = act.reshape(frames * cols, channels)
        before = jnp.where(col == 0, 0.0, pltpu.roll(flat, 1, 0))
        after = jnp.where(col == cols - 1, 0.0, pltpu.roll(flat, frames * cols - 1, 0))
        for kw, part in enumerate((before, flat, after)):
            start = (3 * r + kw) * deep
            taps_ref[:, start : start + channels] = part.astype(jnp.bfloat16)
    outs = []
    for r in range(count):
        lo, hi = max(r - 1, 0), min(r + 1, count - 1)
        left = taps_ref[:, 3 * lo * deep : 3 * (hi + 1) * deep]
        right = w_ref[lo - r + 1 : hi - r + 2]
        right = right.reshape(-1, channels)
        out = jnp.dot(left, right, preferred_element_type=jnp.float32)
        outs.append(out.reshape(frames, cols, channels))
    return outs


def res_kernel(*refs):
    part_refs, (lat_ref, w_out_ref, gn_ref, one_ref, two_ref, out_ref) = refs[:4], refs[4:10]
    comb_ref, taps_ref = refs[10:]
    frames, count, cols, channels = lat_ref.shape
    deep = one_ref.shape[2]
    for i in range(3 * count):
        taps_ref[:, i * deep + channels : (i + 1) * deep] = jnp.zeros(
            (frames * cols, deep - channels), jnp.bfloat16
        )
    size = channels // NORM_GROUPS
    group_r = lax.broadcasted_iota(jnp.int32, (channels, 1), 0) // size
    group_c = lax.broadcasted_iota(jnp.int32, (1, channels), 1) // size
    spread = jnp.where(group_r == group_c, 1.0, 0.0).astype(jnp.bfloat16)
    members = count * cols * size

    core, chip, _ = place()
    half = comb_ref.shape[2] // PACK
    for i, (side, tall) in enumerate(
        ((core, chip), (1 - core, chip), (core, 1 - chip), (1 - core, 1 - chip))
    ):
        for a, piece in enumerate(unpack_lanes(part_refs[i][...].astype(jnp.float32))):
            piece = jnp.concatenate(piece, 1)[:, :channels].astype(jnp.bfloat16)
            comb_ref[:, side * 2 + tall, a * half : (a + 1) * half, :] = piece.reshape(
                frames, half, channels
            )
    combined = comb_ref[...].reshape(frames, count * cols, channels)
    hidden = []
    for r in range(count):
        comb = combined[:, r * cols : (r + 1) * cols, :].reshape(frames * cols, channels)
        proj = jnp.dot(comb, w_out_ref[:channels], preferred_element_type=jnp.float32)
        hid = lat_ref[:, r].astype(jnp.float32) + proj.reshape(frames, cols, channels)
        hidden.append(hid.astype(jnp.bfloat16).astype(jnp.float32))
    acts = group_act(hidden, gn_ref[0:1], spread, members)
    middle = [row + gn_ref[2:3][None] for row in conv_rows(acts, one_ref, taps_ref)]
    acts = group_act(middle, gn_ref[1:2], spread, members)
    for r, row in enumerate(conv_rows(acts, two_ref, taps_ref)):
        out_ref[:, r] = (hidden[r] + row).astype(out_ref.dtype)


def res_block(parts, extras):
    frames, count, cols, channels = extras[0].shape
    deep = -(-channels // LANES) * LANES
    vmem = pl.BlockSpec(memory_space=pltpu.VMEM)
    return pl.pallas_call(
        res_kernel,
        out_shape=jax.ShapeDtypeStruct((frames, count, cols, channels), jnp.bfloat16),
        in_specs=[vmem] * 9,
        out_specs=vmem,
        scratch_shapes=[
            pltpu.VMEM((frames, QUARTERS, count * cols // QUARTERS, channels), jnp.bfloat16),
            pltpu.VMEM((frames * cols, 3 * count * deep), jnp.bfloat16),
        ],
        compiler_params=pltpu.CompilerParams(vmem_limit_bytes=30 * 1024 * 1024),
        name="res_block",
    )(
        *parts,
        *extras,
    )


def body(
    latents, norm_gain, w_qkv, w_out, gn_gain, conv_one, conv_two, step_embed, offsets, numerators
):
    block_len, tile_rows, tile_cols, channels = latents.shape
    planes = lax.axis_size("frame") // QUARTERS
    cells = tile_rows * tile_cols // QUARTERS
    vmem = pl.BlockSpec(memory_space=pltpu.VMEM)
    rows, packed = block_len * cells // PACK, PACK * channels
    near, far = pl.pallas_call(
        pack_kernel,
        out_shape=[jax.ShapeDtypeStruct((2, rows, packed), jnp.bfloat16)] * 2,
        in_specs=[vmem] * 2,
        out_specs=[vmem] * 2,
        name="norm_pack",
    )(latents.reshape(block_len, QUARTERS, cells, channels), norm_gain)
    landed = [
        near,
        moved(far, lambda i: i ^ 2),
        moved(near, lambda i: i + QUARTERS),
        moved(far, lambda i: (i ^ 2) + QUARTERS),
        moved(near, lambda i: i - QUARTERS),
        moved(far, lambda i: (i ^ 2) - QUARTERS),
    ]
    more = (0, -channels % LANES)
    extras = [
        jnp.pad(w_qkv, (more, (0, 0))),
        jnp.concatenate([offsets, numerators]),
        latents,
        jnp.pad(w_out, (more, (0, 0))),
        jnp.concatenate([gn_gain, step_embed[None]]),
        jnp.pad(conv_one, ((0, 0), (0, 0), more, (0, 0))),
        jnp.pad(conv_two, ((0, 0), (0, 0), more, (0, 0))),
    ]
    landed[2], extras = lax.optimization_barrier((landed[2], extras))
    parts = []
    for piece in landed:
        parts += [piece, moved(piece, lambda i: i ^ 1)]
    parts[0] = parts[0][:1]
    w_wide, ints, *extras = extras
    own, sib, far_own, far_sib = attend(parts, w_wide, ints, cells, planes)
    pieces = [
        own,
        moved(sib, lambda i: i ^ 1),
        moved(far_own, lambda i: i ^ 2),
        moved(far_sib, lambda i: i ^ 3),
    ]
    return res_block(pieces, extras)


def solution(mesh):
    return jax.shard_map(
        body,
        mesh=mesh,
        in_specs=(
            P(("groups", "frame"), None, None, None),
            P(),
            P(),
            P(),
            P(),
            P(),
            P(),
            P(),
            P("groups"),
            P(),
        ),
        out_specs=P(("groups", "frame"), None, None, None),
        check_vma=False,
    )
```
